256 devices in a mesh: dp: 32 (over y, x, core), mp: 8 (over z).
Axes of the slice: x: 4, y: 4, z: 8, core: 2. Of those that a mesh axis runs over, the one named last changes fastest.
Arguments:
- query_heads: bfloat16 [32, 1024, 3072], P('dp', None, 'mp'), may hold values from -9 to 9
- key_heads: bfloat16 [32, 1024, 3072], P('dp', None, 'mp'), may hold values from -4.5 to 4.5
- value_heads: bfloat16 [32, 1024, 3072], P('dp', None, 'mp'), may hold values from -4.5 to 4.5
- out_proj: bfloat16 [3072, 6144], P('mp'), may hold values from -0.109375 to 0.109375
- norm_gain: bfloat16 [6144], replicated, may hold values from 0.5 to 1.5
- keep_order: int32 [32, 1024], P('dp'), may hold values from 0 to 1023, each once within a row
- keep_count: int32 [32], replicated, may hold values from 1 to 512, 8192 in all
- cotangent: bfloat16 [32, 1024, 6144], P('dp', None, 'mp'), may hold values from -0.59765625 to 0.59765625
Outputs:
- normed: bfloat16 [32, 1024, 6144], P('dp', None, 'mp')
- grad_query: bfloat16 [32, 1024, 3072], P('dp', None, 'mp')
- grad_key: bfloat16 [32, 1024, 3072], P('dp', None, 'mp')
- grad_value: bfloat16 [32, 1024, 3072], P('dp', None, 'mp')
- grad_out_proj: float32 [3072, 6144], P('mp', 'dp')
The draws below stay inside these ranges and needn't reach their ends.
Inputs may be any that keep to these rules, and one draw needn't show every extreme that they name: `keep_order`: each row holds every token position once. `keep_count`: the counts sum to 8192; the largest is 512.
All inputs are finite; a program needn't handle non-finite values.
Results may differ from the reference program's by a relative error of at most 0.02.
Values may be sent and summed in bfloat16 or wider, within the bound.
No kernel may reach another device: no remote copies, remote signals or barrier semaphores. Data moves between devices by JAX's collectives and lax.ppermute only.
A program may use at most 128 MiB of HBM per device.

```python
import math
import jax
import jax.numpy as jnp
import numpy as np
from jax import lax

D = 6144
HEAD_DIM = 128
P_SIZE = 1024
KEEP_MEAN = 256
KEEP_MAX = 512
IMAGES = 32
HD = 3072


def draw_query_heads(key, part):
    key = jax.random.fold_in(key, 11)
    drawn = jnp.clip(jax.random.normal(key, (IMAGES, P_SIZE, HD), jnp.float32), -4.5, 4.5)
    return drawn.astype(jnp.bfloat16)


def draw_key_heads(key, part):
    key = jax.random.fold_in(key, 12)
    drawn = jnp.clip(jax.random.normal(key, (IMAGES, P_SIZE, HD), jnp.float32), -4.5, 4.5)
    return drawn.astype(jnp.bfloat16)


def strengthened(array, key, source, target, blocks, factor):
    owner, partner = [(jnp.arange(array.shape[axis_at]) // (array.shape[axis_at] // blocks)).reshape([-1 if axis == axis_at else 1 for axis in range(array.ndim)]) for axis_at in (source, target)]
    chosen = jax.random.permutation(key, blocks)[partner]
    strong = (owner == chosen) | (owner == (partner + blocks // 2) % blocks)
    return jnp.where(strong, factor * array, array)


def block_levels(own_key, dims, shards, smallest, top_value):
    level = 1.0
    for dim, shards_of in shards:
        heights = jax.random.uniform(jax.random.fold_in(jax.random.fold_in(own_key, 6), dim), (shards_of,), jnp.float32, smallest / len(shards), top_value / len(shards))
        level = level * jnp.repeat(jnp.exp(heights), dims[dim] // shards_of).reshape((-1,) + (1,) * (len(dims) - 1 - dim))
    return level


def length_profile(amount, total, most, slope):
    portions = [(1 << 20) // math.isqrt(rank ** slope) + 1 for rank in range(2, amount + 1)]
    surplus, counts = total - most - (amount - 1), [1] * (amount - 1)
    while surplus > 0:
        candidates = [i for i in range(amount - 1) if counts[i] < most]
        mass, budget = sum([portions[i] for i in candidates]), surplus
        for i in candidates:
            extra = min(most - counts[i], max(1, budget * portions[i] // mass), surplus)
            counts[i] = counts[i] + extra
            surplus = surplus - extra
    return np.array([most] + counts)


def ragged(own_key, number_of, total, limit, lean):
    if number_of == 2:
        one = jax.random.randint(own_key, (), max(1, total - limit), min(limit, total - 1) + 1)
        return jnp.stack([one, total - one])
    sizes = jnp.asarray(length_profile(number_of, total, limit, lean), jnp.int32)
    pairs = (number_of - 1) // 2
    giver, taker = sizes[1:1 + 2 * pairs:2], sizes[2:2 + 2 * pairs:2]
    slack = jnp.minimum(giver - 1, limit - taker)
    shifted = jax.random.randint(jax.random.fold_in(own_key, 1), (pairs,), 0, 1 << 20) % (slack + 1)
    sizes = sizes.at[1:1 + 2 * pairs:2].set(giver - shifted).at[2:2 + 2 * pairs:2].set(taker + shifted)
    return sizes[jax.random.permutation(jax.random.fold_in(own_key, 2), number_of)]


def normal_values(rng, extent, spread, bound, pieces=(), kind=jnp.bfloat16):
    array = spread * jax.random.normal(rng, extent, jnp.float32)
    if pieces:
        array = array * block_levels(rng, extent, pieces, -0.22, 0.18)
    return jnp.clip(array, -bound, bound).astype(kind)


def bell_draw_with(stream_key, dims, width, bound, split, heavy, kind=jnp.bfloat16):
    array = width * jax.random.normal(stream_key, dims, jnp.float32)
    if split:
        array = array * block_levels(stream_key, dims, split, -0.22, 0.18)
    return jnp.clip(strengthened(array, jax.random.fold_in(stream_key, 3), *heavy), -bound, bound).astype(kind)


def setup_inputs(seed: int = 0) -> dict:
    key_list = jax.random.split(jax.random.key(seed), 9)
    query_heads = draw_query_heads(jax.random.fold_in(key_list[8], 71), 0)
    key_heads = draw_key_heads(jax.random.fold_in(key_list[8], 71), 0)
    value_heads = normal_values(key_list[2], (IMAGES, P_SIZE, HD), 1.0, 4.5, ((0, 32), (2, 8)))
    out_proj = normal_values(key_list[3], (HD, D), HD ** -0.5, 0.109375, ((0, 8),))
    norm_gain = jnp.clip(1.0 + 0.1 * jax.random.normal(key_list[4], (D,), jnp.float32), 0.5, 1.5).astype(jnp.bfloat16)
    keep_order = jax.vmap(lambda own: jax.random.permutation(own, P_SIZE))(jax.random.split(key_list[5], IMAGES)).reshape((IMAGES, P_SIZE)).astype(jnp.int32)
    keep_count = ragged(key_list[6], IMAGES, KEEP_MEAN * IMAGES, KEEP_MAX, 2).astype(jnp.int32)
    cotangent = bell_draw_with(key_list[7], (IMAGES, P_SIZE, D), 0.1, 0.59765625, ((0, 32), (2, 8)), (0, 2, 32, 2.75))
    return {"query_heads": query_heads, "key_heads": key_heads, "value_heads": value_heads, "out_proj": out_proj, "norm_gain": norm_gain, "keep_order": keep_order, "keep_count": keep_count, "cotangent": cotangent}


def attend(query_rows, key_rows, value_rows, live_count):
    row_count = query_rows.shape[0]
    head_count = query_rows.shape[1] // HEAD_DIM
    query_split = query_rows.reshape(row_count, head_count, HEAD_DIM)
    key_split = key_rows.reshape(row_count, head_count, HEAD_DIM)
    value_split = value_rows.reshape(row_count, head_count, HEAD_DIM)
    scores = jnp.einsum('qhd,khd->hqk', query_split, key_split, preferred_element_type=jnp.float32) * HEAD_DIM ** (-0.5)
    live_keys = jnp.arange(row_count) < live_count
    scores = jnp.where(live_keys[None, None, :], scores, -1000000000.0)
    row_max = lax.stop_gradient(lax.optimization_barrier(jnp.max(scores, axis=-1, keepdims=True)))
    exponent = jnp.exp(scores - row_max)
    weights = (exponent / lax.optimization_barrier(jnp.sum(exponent, axis=-1, keepdims=True))).astype(jnp.bfloat16)
    mixed = jnp.einsum('hqk,khd->qhd', weights, value_split, preferred_element_type=jnp.float32)
    return mixed.reshape(row_count, head_count * HEAD_DIM).astype(jnp.bfloat16)

def project(mixed, grad_rows, out_proj, norm_gain):
    projected = jnp.dot(mixed, out_proj, preferred_element_type=jnp.float32)
    row_mean = lax.optimization_barrier(jnp.mean(projected, axis=-1, keepdims=True))
    row_square = lax.optimization_barrier(jnp.mean(projected * projected, axis=-1, keepdims=True))
    inv_std = lax.rsqrt(row_square - row_mean * row_mean + 1e-06)
    centred = (projected - row_mean) * inv_std
    gain_wide = norm_gain.astype(jnp.float32)
    normed = (centred * gain_wide).astype(jnp.bfloat16)
    scaled = grad_rows.astype(jnp.float32) * gain_wide
    first_mean = lax.optimization_barrier(jnp.mean(scaled, axis=-1, keepdims=True))
    second_mean = lax.optimization_barrier(jnp.mean(scaled * centred, axis=-1, keepdims=True))
    grad_proj = (inv_std * (scaled - first_mean - centred * second_mean)).astype(jnp.bfloat16)
    grad_mixed = jnp.dot(grad_proj, out_proj.T, preferred_element_type=jnp.float32).astype(jnp.bfloat16)
    weight_term = jnp.dot(mixed.T, grad_proj, preferred_element_type=jnp.float32)
    return (normed, grad_mixed, weight_term)

def reference(query_heads, key_heads, value_heads, out_proj, norm_gain, keep_order, keep_count, cotangent):

    def one_image(running, inputs):
        query_image, key_image, value_image, order_row, live_count, cotangent_image = inputs
        chosen = order_row[:KEEP_MAX]
        live_rows = jnp.arange(KEEP_MAX) < live_count

        def attend_image(query_part, key_part, value_part):
            return attend(query_part, key_part, value_part, live_count)
        mixed, pullback = jax.vjp(attend_image, query_image[chosen], key_image[chosen], value_image[chosen])
        grad_rows = jnp.where(live_rows[:, None], cotangent_image[chosen], jnp.zeros((), cotangent_image.dtype))
        normed_rows, grad_mixed, weight_term = project(mixed, grad_rows, out_proj, norm_gain)
        normed_rows = jnp.where(live_rows[:, None], normed_rows, jnp.zeros((), normed_rows.dtype))
        grad_query, grad_key, grad_value = pullback(grad_mixed)
        normed_full = jnp.zeros((P_SIZE, normed_rows.shape[1]), normed_rows.dtype).at[chosen].set(normed_rows)
        query_full = jnp.zeros((P_SIZE, grad_query.shape[1]), grad_query.dtype).at[chosen].set(grad_query)
        key_full = jnp.zeros((P_SIZE, grad_key.shape[1]), grad_key.dtype).at[chosen].set(grad_key)
        value_full = jnp.zeros((P_SIZE, grad_value.shape[1]), grad_value.dtype).at[chosen].set(grad_value)
        return (running + weight_term, (normed_full, query_full, key_full, value_full))
    initial = jnp.zeros((HD, D), jnp.float32)
    total, stacked = lax.scan(one_image, initial, (query_heads, key_heads, value_heads, keep_order, keep_count, cotangent))
    return (stacked[0], stacked[1], stacked[2], stacked[3], total)
```

```python
import functools

import jax
import jax.numpy as jnp
from jax import lax
from jax.experimental import pallas as pl
from jax.experimental.pallas import tpu as pltpu
from jax.sharding import PartitionSpec as P

HEAD_DIM = 128
P_SIZE = 1024
KEEP_MAX = 512
VMEM_LIMIT = 56 * 1024 * 1024
BF = jnp.bfloat16
F32 = jnp.float32
STEPS = (0, -1, 1, 2)


def params():
    return pltpu.CompilerParams(vmem_limit_bytes=VMEM_LIMIT)


def call(kernel, grid, prefetched, in_specs, out_specs, out_shape, scratch, *operands):
    return pl.pallas_call(
        kernel,
        grid_spec=pltpu.PrefetchScalarGridSpec(
            num_scalar_prefetch=len(prefetched),
            grid=grid,
            in_specs=in_specs,
            out_specs=out_specs,
            scratch_shapes=scratch,
        ),
        out_shape=out_shape,
        compiler_params=params(),
    )(*prefetched, *operands)


def to_column(row):
    wide = jnp.broadcast_to(row, (128, row.shape[1]))
    return jnp.transpose(wide)[:, :1]


def rows_by_token(order_ref, live):
    token = to_column(order_ref[:, :KEEP_MAX].astype(F32)).astype(jnp.int32)
    row_at = lax.broadcasted_iota(jnp.int32, (KEEP_MAX, P_SIZE), 0)
    token_at = lax.broadcasted_iota(jnp.int32, (KEEP_MAX, P_SIZE), 1)
    return jnp.where((token == token_at) & (row_at < live), 1.0, 0.0).astype(BF)


def tokens_by_row(order_ref, live):
    token_at = lax.broadcasted_iota(jnp.int32, (P_SIZE, KEEP_MAX), 0)
    row_at = lax.broadcasted_iota(jnp.int32, (P_SIZE, KEEP_MAX), 1)
    hit = (order_ref[:, :KEEP_MAX] == token_at) & (row_at < live)
    return jnp.where(hit, 1.0, 0.0).astype(BF)


def dot(a, b, contract):
    return lax.dot_general(a, b, (((contract[0],), (contract[1],)), ((), ())), preferred_element_type=F32)


def attend_kernel(info, counts, order, query, key, value, mixed, query_c, key_c, value_c, weight, pick):
    live = counts[info[0]]

    @pl.when(pl.program_id(0) == 0)
    def _():
        pick[...] = rows_by_token(order, live)

    tokens = jnp.concatenate([query[0], key[0], value[0]], axis=1)
    rows = dot(pick[...], tokens, (1, 0)).astype(BF)
    q, k, v = rows[:, :128], rows[:, 128:256], rows[:, 256:]
    query_c[...], key_c[...], value_c[...] = q, k, v
    scores = dot(q, k, (1, 1)) * HEAD_DIM ** (-0.5)
    column = lax.broadcasted_iota(jnp.int32, (KEEP_MAX, KEEP_MAX), 1)
    scores = jnp.where(column < live, scores, -1000000000.0)
    exponent = jnp.exp(scores - jnp.max(scores, axis=-1, keepdims=True))
    w = exponent / jnp.sum(exponent, axis=-1, keepdims=True)
    weight[0] = w
    mixed[...] = dot(w.astype(BF), v, (1, 0)).astype(BF)


def attend(info, counts, order, query, key, value):
    heads = query.shape[2] // HEAD_DIM
    token_spec = pl.BlockSpec((1, P_SIZE, HEAD_DIM), lambda h, *_: (0, 0, h))
    row_spec = pl.BlockSpec((KEEP_MAX, HEAD_DIM), lambda h, *_: (0, h))
    row_shape = jax.ShapeDtypeStruct((KEEP_MAX, heads * HEAD_DIM), BF)
    return call(
        attend_kernel, (heads,), (info, counts),
        [pl.BlockSpec((1, P_SIZE), lambda h, *_: (0, 0)), token_spec, token_spec, token_spec],
        [row_spec] * 4 + [pl.BlockSpec((1, KEEP_MAX, KEEP_MAX), lambda h, *_: (h, 0, 0))],
        [row_shape] * 4 + [jax.ShapeDtypeStruct((heads, KEEP_MAX, KEEP_MAX), F32)],
        [pltpu.VMEM((KEEP_MAX, P_SIZE), BF)],
        order, query, key, value,
    )


def attend_back_kernel(info, counts, order, grad, query, key, value, weight, grad_q, grad_k, grad_v, place):
    live = counts[info[0]]

    @pl.when(pl.program_id(0) == 0)
    def _():
        place[...] = tokens_by_row(order, live)

    g, q, k, v = grad[...], query[...], key[...], value[...]
    w = weight[0]
    d_weight = dot(g, v, (1, 1)).astype(BF).astype(F32)
    inner = jnp.sum(d_weight * w, axis=-1, keepdims=True)
    d_scores = (w * (d_weight - inner) * HEAD_DIM ** (-0.5)).astype(BF)
    dq = dot(d_scores, k, (1, 0)).astype(BF)
    dk = dot(d_scores, q, (0, 0)).astype(BF)
    dv = dot(w.astype(BF), g, (0, 0)).astype(BF)
    out = dot(place[...], jnp.concatenate([dq, dk, dv], axis=1), (1, 0)).astype(BF)
    grad_q[0], grad_k[0], grad_v[0] = out[:, :128], out[:, 128:256], out[:, 256:]


def attend_back(info, counts, order, grad, query, key, value, weight):
    heads = query.shape[1] // HEAD_DIM
    token_spec = pl.BlockSpec((1, P_SIZE, HEAD_DIM), lambda h, *_: (0, 0, h))
    row_spec = pl.BlockSpec((KEEP_MAX, HEAD_DIM), lambda h, *_: (0, h))
    token_shape = jax.ShapeDtypeStruct((1, P_SIZE, heads * HEAD_DIM), BF)
    return call(
        attend_back_kernel, (heads,), (info, counts),
        [pl.BlockSpec((1, P_SIZE), lambda h, *_: (0, 0))] + [row_spec] * 4
        + [pl.BlockSpec((1, KEEP_MAX, KEEP_MAX), lambda h, *_: (h, 0, 0))],
        [token_spec] * 3, [token_shape] * 3,
        [pltpu.VMEM((P_SIZE, KEEP_MAX), BF)],
        order, grad, query, key, value, weight,
    )


def pick_kernel(info, counts, order, tokens, rows, pick):
    @pl.when(pl.program_id(0) == 0)
    def _():
        pick[...] = rows_by_token(order, counts[info[0]])

    rows[...] = dot(pick[...], tokens[0], (1, 0)).astype(BF)


def pick_rows(info, counts, order, tokens):
    width = tokens.shape[2]
    return call(
        pick_kernel, (width // 256,), (info, counts),
        [pl.BlockSpec((1, P_SIZE), lambda j, *_: (0, 0)), pl.BlockSpec((1, P_SIZE, 256), lambda j, *_: (0, 0, j))],
        pl.BlockSpec((KEEP_MAX, 256), lambda j, *_: (0, j)),
        jax.ShapeDtypeStruct((KEEP_MAX, width), BF),
        [pltpu.VMEM((KEEP_MAX, P_SIZE), BF)],
        order, tokens,
    )


def place_kernel(info, counts, order, rows, tokens, place):
    @pl.when(pl.program_id(0) == 0)
    def _():
        place[...] = tokens_by_row(order, counts[info[0]])

    tokens[0] = dot(place[...], rows[...], (1, 0)).astype(BF)


def place_rows(info, counts, order, rows):
    width = rows.shape[1]
    return call(
        place_kernel, (width // 256,), (info, counts),
        [pl.BlockSpec((1, P_SIZE), lambda j, *_: (0, 0)), pl.BlockSpec((KEEP_MAX, 256), lambda j, *_: (0, j))],
        pl.BlockSpec((1, P_SIZE, 256), lambda j, *_: (0, 0, j)),
        jax.ShapeDtypeStruct((1, P_SIZE, width), BF),
        [pltpu.VMEM((P_SIZE, KEEP_MAX), BF)],
        order, rows,
    )


def cut_kernel(info, left, right, out):
    half = left.shape[1]
    out[0, :, :half] = left[...]
    out[0, :, half:] = right[...]


def assemble_kernel(info, *refs):
    out = refs[-1]
    half = out.shape[2] // 2
    rows = out.shape[1]
    part = rows // 8
    for stream in range(2):
        place = info[2 + stream]
        for at, step in enumerate(STEPS):
            quarter = lax.rem(place + 4 + step, 4)
            for core in range(2):
                piece = refs[(stream * 4 + at) * 2 + core]
                side = jnp.where(core == 0, info[4], 1 - info[4])
                start = pl.multiple_of((side * 4 + quarter) * part, 16)
                out[0, pl.ds(start, part), pl.ds(stream * half, half)] = piece[0]


def gather_columns(info, out_proj, permute_tables):
    rows, full = out_proj.shape
    ranks = lax.axis_size("mp")
    width = full // ranks
    half, part = width // 2, rows // 8
    cut = call(
        cut_kernel, (ranks,), (info,),
        [
            pl.BlockSpec((part, half), lambda m, i: (i[4] * 4 + i[2], 2 * m)),
            pl.BlockSpec((part, half), lambda m, i: (i[4] * 4 + i[3], 2 * m + 1)),
        ],
        pl.BlockSpec((1, part, width), lambda m, i: (m, 0, 0)),
        jax.ShapeDtypeStruct((ranks, part, width), BF), [],
        out_proj, out_proj,
    )
    got = lax.all_to_all(cut, "mp", split_axis=0, concat_axis=0, tiled=True)
    pieces = []
    for stream in range(2):
        own = got[:, :, stream * half:(stream + 1) * half]
        for step in STEPS:
            piece = own if step == 0 else lax.ppermute(own, "dp", permute_tables[stream][step])
            pieces += [piece, lax.ppermute(piece, "dp", permute_tables[2])]
    piece_spec = pl.BlockSpec((1, part, half), lambda m, i: (m, 0, 0))
    whole = call(
        assemble_kernel, (ranks,), (info,),
        [piece_spec] * 16,
        pl.BlockSpec((1, rows, width), lambda m, i: (m, 0, 0)),
        jax.ShapeDtypeStruct((ranks, rows, width), BF), [],
        *pieces,
    )
    return whole.reshape(ranks * rows, width)


def project_kernel(info, mixed, weight, grad, gain, projected, sums):
    step = pl.program_id(0)
    part = dot(mixed[...], weight[...], (1, 0))

    @pl.when(step == 0)
    def _():
        projected[...] = part

    @pl.when(step > 0)
    def _():
        projected[...] += part

    @pl.when(step == pl.num_programs(0) - 1)
    def _():
        values = projected[...]
        scaled = grad[...].astype(F32) * gain[...].astype(F32)
        lane = lax.broadcasted_iota(jnp.int32, (KEEP_MAX, 128), 1)
        table = jnp.zeros((KEEP_MAX, 128), F32)
        for at, term in enumerate((values, values * values, scaled, scaled * values)):
            table = jnp.where(lane == at, jnp.sum(term, axis=-1, keepdims=True), table)
        sums[...] = jnp.transpose(table)[:8]


def project(info, mixed, weight, grad, gain):
    depth, width = weight.shape
    block = 768
    return call(
        project_kernel, (depth // block,), (info,),
        [
            pl.BlockSpec((KEEP_MAX, block), lambda k, i: (0, k)),
            pl.BlockSpec((block, width), lambda k, i: (k, 0)),
            pl.BlockSpec((KEEP_MAX, width), lambda k, i: (0, 0)),
            pl.BlockSpec((1, width), lambda k, i: (0, i[1])),
        ],
        [pl.BlockSpec((KEEP_MAX, width), lambda k, i: (0, 0)), pl.BlockSpec((8, KEEP_MAX), lambda k, i: (0, 0))],
        [jax.ShapeDtypeStruct((KEEP_MAX, width), F32), jax.ShapeDtypeStruct((8, KEEP_MAX), F32)],
        [], mixed, weight, grad, gain,
    )


def grad_kernel(full_width, info, counts, projected, grad, gain, weight, *refs):
    *sums, out, grad_proj, normed = refs

    @pl.when(pl.program_id(0) == 0)
    def _():
        total = sums[0][...]
        for other in sums[1:]:
            total = total + other[...]
        total = jnp.concatenate([total, jnp.zeros((120, KEEP_MAX), F32)], axis=0)
        table = jnp.transpose(total) / full_width
        row_mean, row_square, first, cross = (table[:, at:at + 1] for at in range(4))
        inv_std = lax.rsqrt(row_square - row_mean * row_mean + 1e-06)
        second = (cross - row_mean * first) * inv_std
        live = lax.broadcasted_iota(jnp.int32, (KEEP_MAX, 1), 0) < counts[info[0]]
        gain_wide = gain[...].astype(F32)
        centred = (projected[...] - row_mean) * inv_std
        scaled = grad[...].astype(F32) * gain_wide
        normed[...] = jnp.where(live, centred * gain_wide, 0.0).astype(BF)
        grad_proj[...] = jnp.where(live, inv_std * (scaled - first - centred * second), 0.0).astype(BF)

    product = dot(grad_proj[...], weight[...], (1, 1)).astype(BF)
    half = out.shape[2]
    out[0] = product[:, :half]
    out[1] = product[:, half:]


def grad_rows(info, counts, projected, grad, gain, weight, sums, full_width):
    depth, width = weight.shape
    block = 768
    whole = pl.BlockSpec((KEEP_MAX, width), lambda k, *i: (0, 0))
    rows_shape = jax.ShapeDtypeStruct((KEEP_MAX, width), BF)
    return call(
        functools.partial(grad_kernel, full_width), (depth // block,), (info, counts),
        [
            whole, whole,
            pl.BlockSpec((1, width), lambda k, i, c: (0, i[1])),
            pl.BlockSpec((block, width), lambda k, *i: (k, 0)),
        ] + [pl.BlockSpec((8, KEEP_MAX), lambda k, *i: (0, 0))] * len(sums),
        [pl.BlockSpec((2, KEEP_MAX, block // 2), lambda k, *i: (k, 0, 0)), whole, whole],
        [jax.ShapeDtypeStruct((depth * 2 // block, KEEP_MAX, block // 2), BF), rows_shape, rows_shape],
        [], projected, grad, gain, weight, *sums,
    )


def outer_kernel(info, grad_proj, mixed, out, turned):
    @pl.when(pl.program_id(0) == 0)
    def _():
        turned[...] = jnp.transpose(grad_proj[...])

    out[0] = dot(turned[...], mixed[...], (1, 0)).astype(BF)


def outer(info, grad_proj, mixed, keep):
    width = grad_proj.shape[1]
    block = mixed.shape[1] // 8

    def at(j, i):
        side = i[4] if keep else 1 - i[4]
        return 0, side * 4 + j

    return call(
        outer_kernel, (4,), (info,),
        [pl.BlockSpec((KEEP_MAX, width), lambda j, i: (0, 0)), pl.BlockSpec((KEEP_MAX, block), at)],
        pl.BlockSpec((1, width, block), lambda j, i: (j, 0, 0)),
        jax.ShapeDtypeStruct((4, width, block), BF),
        [pltpu.VMEM((width, KEEP_MAX), BF)],
        grad_proj, mixed,
    )


def dp_index(y, x, core):
    return (y % 4) * 8 + (x % 4) * 2 + core


def on_device(
    query_heads, key_heads, value_heads, out_proj, norm_gain, keep_order, keep_count, cotangent
):
    ranks = lax.axis_size("mp")
    image = lax.axis_index("dp")
    rank = lax.axis_index("mp")
    info = jnp.stack([image, rank, image // 8, (image // 2) % 4, image % 2]).astype(jnp.int32)
    chips = [(y, x, core) for y in range(4) for x in range(4) for core in range(2)]
    tables = (
        {s: [(dp_index(y, x, c), dp_index(y - s, x, c)) for y, x, c in chips] for s in STEPS[1:]},
        {s: [(dp_index(y, x, c), dp_index(y, x - s, c)) for y, x, c in chips] for s in STEPS[1:]},
        [(dp_index(y, x, c), dp_index(y, x, 1 - c)) for y, x, c in chips],
    )
    gain = norm_gain.reshape(1, -1)

    columns = gather_columns(info, out_proj, tables)
    mixed, query_c, key_c, value_c, weights = attend(
        info, keep_count, keep_order, query_heads, key_heads, value_heads
    )
    mixed_all = lax.all_gather(mixed, "mp", axis=1, tiled=True)
    grad_c = pick_rows(info, keep_count, keep_order, cotangent)
    projected, sums = project(info, mixed_all, columns, grad_c, gain)
    all_sums = [sums] + [
        lax.ppermute(sums, "mp", [(m, (m + s) % ranks) for m in range(ranks)]) for s in range(1, ranks)
    ]
    mixed_grad, grad_proj, normed_c = grad_rows(
        info, keep_count, projected, grad_c, gain, columns, all_sums, norm_gain.shape[0]
    )
    grad_mixed = lax.psum_scatter(mixed_grad, "mp", scatter_dimension=0, tiled=True)[0]

    sent = outer(info, grad_proj, mixed_all, False)
    other = lax.ppermute(sent, "dp", tables[2])
    kept = outer(info, grad_proj, mixed_all, True)
    width, depth = kept.shape[1], kept.shape[2]
    pair = (kept.astype(F32) + other.astype(F32)).astype(BF).reshape(16, width // 4, depth)
    groups = [[2 * j + c for j in range(16)] for c in range(2)]
    spread = lax.all_to_all(
        pair, "dp", split_axis=0, concat_axis=0, tiled=True, axis_index_groups=groups
    )
    total = jnp.sum(spread.astype(F32), axis=0).astype(BF)
    home = [
        (dp_index(y, x, c) * ranks + m, (4 * m + x) * ranks + 4 * c + y)
        for y, x, c in chips for m in range(ranks)
    ]
    weight_grad = lax.ppermute(total, ("dp", "mp"), home).astype(F32).T

    normed = place_rows(info, keep_count, keep_order, normed_c)
    grads = attend_back(info, keep_count, keep_order, grad_mixed, query_c, key_c, value_c, weights)
    return (normed, *grads, weight_grad)


def solution(mesh):
    in_specs = (
        P("dp", None, "mp"),
        P("dp", None, "mp"),
        P("dp", None, "mp"),
        P("mp", None),
        P(),
        P("dp", None),
        P(),
        P("dp", None, "mp"),
    )
    out_specs = (
        P("dp", None, "mp"),
        P("dp", None, "mp"),
        P("dp", None, "mp"),
        P("dp", None, "mp"),
        P("mp", "dp"),
    )
    return jax.shard_map(
        on_device, mesh=mesh, in_specs=in_specs, out_specs=out_specs, check_vma=False
    )
```

```python
import functools

import jax
import jax.numpy as jnp
from jax import lax
from jax.experimental import pallas as pl
from jax.experimental.pallas import tpu as pltpu
from jax.sharding import PartitionSpec as P

HEAD_DIM = 128
P_SIZE = 1024
KEEP_MAX = 512
VMEM_LIMIT = 56 * 1024 * 1024
BF = jnp.bfloat16
F32 = jnp.float32
STEPS = (0, -1, 1, 2)


def params():
    return pltpu.CompilerParams(vmem_limit_bytes=VMEM_LIMIT)


def call(kernel, grid, prefetched, in_specs, out_specs, out_shape, scratch, *operands, flops=0):
    moved = sum(a.size * a.dtype.itemsize for a in jax.tree.leaves((operands, out_shape)))
    return pl.pallas_call(
        kernel,
        grid_spec=pltpu.PrefetchScalarGridSpec(
            num_scalar_prefetch=len(prefetched),
            grid=grid,
            in_specs=in_specs,
            out_specs=out_specs,
            scratch_shapes=scratch,
        ),
        out_shape=out_shape,
        compiler_params=params(),
        cost_estimate=pl.CostEstimate(flops=flops, bytes_accessed=moved, transcendentals=0),
    )(*prefetched, *operands)


def to_column(row):
    wide = jnp.broadcast_to(row, (128, row.shape[1]))
    return jnp.transpose(wide)[:, :1]


def rows_by_token(order_ref, live):
    token = to_column(order_ref[:, :KEEP_MAX].astype(F32)).astype(jnp.int32)
    row_at = lax.broadcasted_iota(jnp.int32, (KEEP_MAX, P_SIZE), 0)
    token_at = lax.broadcasted_iota(jnp.int32, (KEEP_MAX, P_SIZE), 1)
    return jnp.where((token == token_at) & (row_at < live), 1.0, 0.0).astype(BF)


def tokens_by_row(order_ref, live):
    token_at = lax.broadcasted_iota(jnp.int32, (P_SIZE, KEEP_MAX), 0)
    row_at = lax.broadcasted_iota(jnp.int32, (P_SIZE, KEEP_MAX), 1)
    hit = (order_ref[:, :KEEP_MAX] == token_at) & (row_at < live)
    return jnp.where(hit, 1.0, 0.0).astype(BF)


def dot(a, b, contract):
    return lax.dot_general(a, b, (((contract[0],), (contract[1],)), ((), ())), preferred_element_type=F32)


def attend_kernel(info, counts, order, query, key, value, mixed, query_c, key_c, value_c, weight, pick):
    live = counts[info[0]]

    @pl.when(pl.program_id(0) == 0)
    def _():
        pick[...] = rows_by_token(order, live)

    tokens = jnp.concatenate([query[0], key[0], value[0]], axis=1)
    rows = dot(pick[...], tokens, (1, 0)).astype(BF)
    q, k, v = rows[:, :128], rows[:, 128:256], rows[:, 256:]
    query_c[...], key_c[...], value_c[...] = q, k, v
    scores = dot(q, k, (1, 1)) * HEAD_DIM ** (-0.5)
    column = lax.broadcasted_iota(jnp.int32, (KEEP_MAX, KEEP_MAX), 1)
    scores = jnp.where(column < live, scores, -1000000000.0)
    exponent = jnp.exp(scores - jnp.max(scores, axis=-1, keepdims=True))
    w = exponent / jnp.sum(exponent, axis=-1, keepdims=True)
    weight[0] = w
    mixed[...] = dot(w.astype(BF), v, (1, 0)).astype(BF)


def attend(info, counts, order, query, key, value):
    heads = query.shape[2] // HEAD_DIM
    token_spec = pl.BlockSpec((1, P_SIZE, HEAD_DIM), lambda h, *_: (0, 0, h))
    row_spec = pl.BlockSpec((KEEP_MAX, HEAD_DIM), lambda h, *_: (0, h))
    row_shape = jax.ShapeDtypeStruct((KEEP_MAX, heads * HEAD_DIM), BF)
    return call(
        attend_kernel, (heads,), (info, counts),
        [pl.BlockSpec((1, P_SIZE), lambda h, *_: (0, 0)), token_spec, token_spec, token_spec],
        [row_spec] * 4 + [pl.BlockSpec((1, KEEP_MAX, KEEP_MAX), lambda h, *_: (h, 0, 0))],
        [row_shape] * 4 + [jax.ShapeDtypeStruct((heads, KEEP_MAX, KEEP_MAX), F32)],
        [pltpu.VMEM((KEEP_MAX, P_SIZE), BF)],
        order, query, key, value,
    )


def attend_back_kernel(info, counts, order, grad, query, key, value, weight, grad_q, grad_k, grad_v, place):
    live = counts[info[0]]

    @pl.when(pl.program_id(0) == 0)
    def _():
        place[...] = tokens_by_row(order, live)

    g, q, k, v = grad[...], query[...], key[...], value[...]
    w = weight[0]
    d_weight = dot(g, v, (1, 1)).astype(BF).astype(F32)
    inner = jnp.sum(d_weight * w, axis=-1, keepdims=True)
    d_scores = (w * (d_weight - inner) * HEAD_DIM ** (-0.5)).astype(BF)
    dq = dot(d_scores, k, (1, 0)).astype(BF)
    dk = dot(d_scores, q, (0, 0)).astype(BF)
    dv = dot(w.astype(BF), g, (0, 0)).astype(BF)
    out = dot(place[...], jnp.concatenate([dq, dk, dv], axis=1), (1, 0)).astype(BF)
    grad_q[0], grad_k[0], grad_v[0] = out[:, :128], out[:, 128:256], out[:, 256:]


def attend_back(info, counts, order, grad, query, key, value, weight):
    heads = query.shape[1] // HEAD_DIM
    token_spec = pl.BlockSpec((1, P_SIZE, HEAD_DIM), lambda h, *_: (0, 0, h))
    row_spec = pl.BlockSpec((KEEP_MAX, HEAD_DIM), lambda h, *_: (0, h))
    token_shape = jax.ShapeDtypeStruct((1, P_SIZE, heads * HEAD_DIM), BF)
    return call(
        attend_back_kernel, (heads,), (info, counts),
        [pl.BlockSpec((1, P_SIZE), lambda h, *_: (0, 0))] + [row_spec] * 4
        + [pl.BlockSpec((1, KEEP_MAX, KEEP_MAX), lambda h, *_: (h, 0, 0))],
        [token_spec] * 3, [token_shape] * 3,
        [pltpu.VMEM((P_SIZE, KEEP_MAX), BF)],
        order, grad, query, key, value, weight,
    )


def pick_kernel(info, counts, order, tokens, rows, pick):
    @pl.when(pl.program_id(0) == 0)
    def _():
        pick[...] = rows_by_token(order, counts[info[0]])

    rows[...] = dot(pick[...], tokens[0], (1, 0)).astype(BF)


def pick_rows(info, counts, order, tokens):
    width = tokens.shape[2]
    return call(
        pick_kernel, (width // 256,), (info, counts),
        [pl.BlockSpec((1, P_SIZE), lambda j, *_: (0, 0)), pl.BlockSpec((1, P_SIZE, 256), lambda j, *_: (0, 0, j))],
        pl.BlockSpec((KEEP_MAX, 256), lambda j, *_: (0, j)),
        jax.ShapeDtypeStruct((KEEP_MAX, width), BF),
        [pltpu.VMEM((KEEP_MAX, P_SIZE), BF)],
        order, tokens,
    )


def place_kernel(info, counts, order, rows, tokens, place):
    @pl.when(pl.program_id(0) == 0)
    def _():
        place[...] = tokens_by_row(order, counts[info[0]])

    tokens[0] = dot(place[...], rows[...], (1, 0)).astype(BF)


def place_rows(info, counts, order, rows):
    width = rows.shape[1]
    return call(
        place_kernel, (width // 256,), (info, counts),
        [pl.BlockSpec((1, P_SIZE), lambda j, *_: (0, 0)), pl.BlockSpec((KEEP_MAX, 256), lambda j, *_: (0, j))],
        pl.BlockSpec((1, P_SIZE, 256), lambda j, *_: (0, 0, j)),
        jax.ShapeDtypeStruct((1, P_SIZE, width), BF),
        [pltpu.VMEM((P_SIZE, KEEP_MAX), BF)],
        order, rows,
    )


def cut_kernel(info, left, right, out):
    ranks, _, width = out.shape
    half = width // 2
    for m in range(ranks):
        out[m, :, :half] = left[:, m * width:m * width + half]
        out[m, :, half:] = right[:, m * width + half:(m + 1) * width]


def assemble_kernel(info, *refs):
    *pieces, out = refs
    _, rows, width = out.shape
    half, part = width // 2, rows // 8
    for stream in range(2):
        for at, step in enumerate(STEPS):
            quarter = lax.rem(info[2 + stream] + 4 + step, 4)
            for core in range(2):
                side = info[4] if core == 0 else 1 - info[4]
                start = pl.multiple_of((side * 4 + quarter) * part, 16)
                piece = pieces[(stream * 4 + at) * 2 + core]
                out[:, pl.ds(start, part), stream * half:(stream + 1) * half] = piece[...]


def gather_columns(info, out_proj, chips):
    rows, full = out_proj.shape
    ranks = lax.axis_size("mp")
    width = full // ranks
    half, part = width // 2, rows // 8
    cut = call(
        cut_kernel, (1,), (info,),
        [
            pl.BlockSpec((part, full), lambda _, i: (i[4] * 4 + i[2], 0)),
            pl.BlockSpec((part, full), lambda _, i: (i[4] * 4 + i[3], 0)),
        ],
        pl.BlockSpec((ranks, part, width), lambda _, i: (0, 0, 0)),
        jax.ShapeDtypeStruct((ranks, part, width), BF), [],
        out_proj, out_proj,
    )
    got = lax.all_to_all(cut, "mp", split_axis=0, concat_axis=0, tiled=True)
    swap = [(dp_index(y, x, c), dp_index(y, x, 1 - c)) for y, x, c in chips]
    pieces = []
    for stream in range(2):
        own = got[:, :, stream * half:(stream + 1) * half]
        for s in STEPS:
            if stream == 0:
                table = [(dp_index(y, x, c), dp_index(y - s, x, c)) for y, x, c in chips]
            else:
                table = [(dp_index(y, x, c), dp_index(y, x - s, c)) for y, x, c in chips]
            piece = own if s == 0 else lax.ppermute(own, "dp", table)
            pieces += [piece, lax.ppermute(piece, "dp", swap)]
    steps = 2
    whole = call(
        assemble_kernel, (steps,), (info,),
        [pl.BlockSpec((ranks // steps, part, half), lambda m, i: (m, 0, 0))] * 16,
        pl.BlockSpec((ranks // steps, rows, width), lambda m, i: (m, 0, 0)),
        jax.ShapeDtypeStruct((ranks, rows, width), BF), [],
        *pieces,
    )
    return cut, whole.reshape(ranks * rows, width)


def project_kernel(info, mixed, weight, grad, gain, projected, sums):
    step = pl.program_id(0)
    part = dot(mixed[...], weight[...], (1, 0))

    @pl.when(step == 0)
    def _():
        projected[...] = part

    @pl.when(step > 0)
    def _():
        projected[...] += part

    @pl.when(step == pl.num_programs(0) - 1)
    def _():
        values = projected[...]
        scaled = grad[...].astype(F32) * gain[...].astype(F32)
        lane = lax.broadcasted_iota(jnp.int32, (KEEP_MAX, 128), 1)
        table = jnp.zeros((KEEP_MAX, 128), F32)
        for at, term in enumerate((values, values * values, scaled, scaled * values)):
            table = jnp.where(lane == at, jnp.sum(term, axis=-1, keepdims=True), table)
        sums[...] = jnp.transpose(table)[:8]


def project(info, mixed, weight, grad, gain):
    depth, width = weight.shape
    block = 768
    return call(
        project_kernel, (depth // block,), (info,),
        [
            pl.BlockSpec((KEEP_MAX, block), lambda k, i: (0, k)),
            pl.BlockSpec((block, width), lambda k, i: (k, 0)),
            pl.BlockSpec((KEEP_MAX, width), lambda k, i: (0, 0)),
            pl.BlockSpec((1, width), lambda k, i: (0, i[1])),
        ],
        [pl.BlockSpec((KEEP_MAX, width), lambda k, i: (0, 0)), pl.BlockSpec((8, KEEP_MAX), lambda k, i: (0, 0))],
        [jax.ShapeDtypeStruct((KEEP_MAX, width), F32), jax.ShapeDtypeStruct((8, KEEP_MAX), F32)],
        [], mixed, weight, grad, gain,
    )


def grad_kernel(full_width, info, counts, projected, grad, gain, weight, *refs):
    *sums, out, grad_proj, normed = refs

    @pl.when(pl.program_id(0) == 0)
    def _():
        total = sums[0][...]
        for other in sums[1:]:
            total = total + other[...]
        total = jnp.concatenate([total, jnp.zeros((120, KEEP_MAX), F32)], axis=0)
        table = jnp.transpose(total) / full_width
        row_mean, row_square, first, cross = (table[:, at:at + 1] for at in range(4))
        inv_std = lax.rsqrt(row_square - row_mean * row_mean + 1e-06)
        second = (cross - row_mean * first) * inv_std
        live = lax.broadcasted_iota(jnp.int32, (KEEP_MAX, 1), 0) < counts[info[0]]
        gain_wide = gain[...].astype(F32)
        centred = (projected[...] - row_mean) * inv_std
        scaled = grad[...].astype(F32) * gain_wide
        normed[...] = jnp.where(live, centred * gain_wide, 0.0).astype(BF)
        grad_proj[...] = jnp.where(live, inv_std * (scaled - first - centred * second), 0.0).astype(BF)

    product = dot(grad_proj[...], weight[...], (1, 1)).astype(BF)
    half = out.shape[2]
    out[0] = product[:, :half]
    out[1] = product[:, half:]


def grad_rows(info, counts, projected, grad, gain, weight, sums, full_width):
    depth, width = weight.shape
    block = 768
    whole = pl.BlockSpec((KEEP_MAX, width), lambda k, *i: (0, 0))
    rows_shape = jax.ShapeDtypeStruct((KEEP_MAX, width), BF)
    return call(
        functools.partial(grad_kernel, full_width), (depth // block,), (info, counts),
        [
            whole, whole,
            pl.BlockSpec((1, width), lambda k, i, c: (0, i[1])),
            pl.BlockSpec((block, width), lambda k, *i: (k, 0)),
        ] + [pl.BlockSpec((8, KEEP_MAX), lambda k, *i: (0, 0))] * len(sums),
        [pl.BlockSpec((2, KEEP_MAX, block // 2), lambda k, *i: (k, 0, 0)), whole, whole],
        [jax.ShapeDtypeStruct((depth * 2 // block, KEEP_MAX, block // 2), BF), rows_shape, rows_shape],
        [], projected, grad, gain, weight, *sums,
    )


def outer_kernel(info, own_grad, other_grad, own_mixed, other_mixed, out, turned):
    @pl.when(pl.program_id(0) == 0)
    def _():
        turned[:, :KEEP_MAX] = jnp.transpose(own_grad[...])
        turned[:, KEEP_MAX:] = jnp.transpose(other_grad[...])

    rows = jnp.concatenate([own_mixed[...], other_mixed[...]], axis=0)
    out[0] = dot(turned[...], rows, (1, 0)).astype(BF)


def outer(info, own_grad, other_grad, mixed, other_mixed):
    width = own_grad.shape[1]
    block = mixed.shape[1] // 8
    grad_spec = pl.BlockSpec((KEEP_MAX, width), lambda j, i: (0, 0))
    return call(
        outer_kernel, (4,), (info,),
        [
            grad_spec, grad_spec,
            pl.BlockSpec((KEEP_MAX, block), lambda j, i: (0, i[4] * 4 + j)),
            pl.BlockSpec((KEEP_MAX, block), lambda j, i: (0, j)),
        ],
        pl.BlockSpec((1, width, block), lambda j, i: (j, 0, 0)),
        jax.ShapeDtypeStruct((4, width, block), BF),
        [pltpu.VMEM((width, 2 * KEEP_MAX), BF)],
        own_grad, other_grad, mixed, other_mixed,
    )


def dp_index(y, x, core):
    return (y % 4) * 8 + (x % 4) * 2 + core


def on_device(
    query_heads, key_heads, value_heads, out_proj, norm_gain, keep_order, keep_count, cotangent
):
    ranks = lax.axis_size("mp")
    image = lax.axis_index("dp")
    rank = lax.axis_index("mp")
    info = jnp.stack([image, rank, image // 8, (image // 2) % 4, image % 2]).astype(jnp.int32)
    chips = [(y, x, core) for y in range(4) for x in range(4) for core in range(2)]
    swap = [(dp_index(y, x, c), dp_index(y, x, 1 - c)) for y, x, c in chips]
    gain = norm_gain.reshape(1, -1)

    cut, columns = gather_columns(info, out_proj, chips)
    early, _ = lax.optimization_barrier((info, cut))
    mixed, query_c, key_c, value_c, weights = attend(
        early, keep_count, keep_order, query_heads, key_heads, value_heads
    )
    mixed_all = lax.all_gather(mixed, "mp", axis=1, tiled=True)
    late, _ = lax.optimization_barrier((info, columns))
    grad_c = pick_rows(late, keep_count, keep_order, cotangent)
    projected, sums = project(info, mixed_all, columns, grad_c, gain)
    pair_sums = sums + lax.ppermute(sums, "mp", [(m, m ^ 1) for m in range(ranks)])
    all_sums = [pair_sums] + [
        lax.ppermute(pair_sums, "mp", [(m, m ^ s) for m in range(ranks)]) for s in range(2, ranks, 2)
    ]
    half = mixed_all.shape[1] // 2
    sent_mixed = lax.dynamic_slice_in_dim(mixed_all, (1 - image % 2) * half, half, 1)
    other_mixed = lax.ppermute(sent_mixed, "dp", swap)
    all_sums, other_mixed = lax.optimization_barrier((all_sums, other_mixed))
    mixed_grad, grad_proj, normed_c = grad_rows(
        info, keep_count, projected, grad_c, gain, columns, all_sums, norm_gain.shape[0]
    )
    grad_mixed = lax.psum_scatter(mixed_grad, "mp", scatter_dimension=0, tiled=True)[0]

    other_grad = lax.ppermute(grad_proj, "dp", swap)
    normed = place_rows(info, keep_count, keep_order, normed_c)
    other_grad, normed = lax.optimization_barrier((other_grad, normed))
    pair = outer(info, grad_proj, other_grad, mixed_all, other_mixed)
    width, depth = pair.shape[1], pair.shape[2]
    pair = pair.reshape(16, width // 4, depth)
    groups = [[2 * j + c for j in range(16)] for c in range(2)]
    spread = lax.all_to_all(
        pair, "dp", split_axis=0, concat_axis=0, tiled=True, axis_index_groups=groups
    )
    total = jnp.sum(spread.astype(F32), axis=0).astype(BF)
    home = [
        (dp_index(y, x, c) * ranks + m, (4 * m + x) * ranks + 4 * c + y)
        for y, x, c in chips for m in range(ranks)
    ]
    total = lax.ppermute(total, ("dp", "mp"), home)

    grads = attend_back(info, keep_count, keep_order, grad_mixed, query_c, key_c, value_c, weights)
    total, grads = lax.optimization_barrier((total, grads))
    return (normed, *grads, total.astype(F32).T)


def solution(mesh):
    in_specs = (
        P("dp", None, "mp"),
        P("dp", None, "mp"),
        P("dp", None, "mp"),
        P("mp", None),
        P(),
        P("dp", None),
        P(),
        P("dp", None, "mp"),
    )
    out_specs = (
        P("dp", None, "mp"),
        P("dp", None, "mp"),
        P("dp", None, "mp"),
        P("dp", None, "mp"),
        P("mp", "dp"),
    )
    return jax.shard_map(
        on_device, mesh=mesh, in_specs=in_specs, out_specs=out_specs, check_vma=False
    )
```

```python
import functools

import jax
import jax.numpy as jnp
from jax import lax
from jax.experimental import pallas as pl
from jax.experimental.pallas import tpu as pltpu
from jax.sharding import PartitionSpec as P

HEAD_DIM = 128
P_SIZE = 1024
KEEP_MAX = 512
VMEM_LIMIT = 56 * 1024 * 1024
BF = jnp.bfloat16
F32 = jnp.float32
STEPS = (0, -1, 1, 2)


def params():
    return pltpu.CompilerParams(vmem_limit_bytes=VMEM_LIMIT)


def call(kernel, grid, prefetched, in_specs, out_specs, out_shape, scratch, *operands, flops=0):
    moved = sum(a.size * a.dtype.itemsize for a in jax.tree.leaves((operands, out_shape)))
    return pl.pallas_call(
        kernel,
        grid_spec=pltpu.PrefetchScalarGridSpec(
            num_scalar_prefetch=len(prefetched),
            grid=grid,
            in_specs=in_specs,
            out_specs=out_specs,
            scratch_shapes=scratch,
        ),
        out_shape=out_shape,
        compiler_params=params(),
        cost_estimate=pl.CostEstimate(flops=flops, bytes_accessed=moved, transcendentals=0),
    )(*prefetched, *operands)


def to_column(row):
    wide = jnp.broadcast_to(row, (128, row.shape[1]))
    return jnp.transpose(wide)[:, :1]


def rows_by_token(order_ref, live):
    token = to_column(order_ref[:, :KEEP_MAX].astype(F32)).astype(jnp.int32)
    row_at = lax.broadcasted_iota(jnp.int32, (KEEP_MAX, P_SIZE), 0)
    token_at = lax.broadcasted_iota(jnp.int32, (KEEP_MAX, P_SIZE), 1)
    return jnp.where((token == token_at) & (row_at < live), 1.0, 0.0).astype(BF)


def tokens_by_row(order_ref, live):
    token_at = lax.broadcasted_iota(jnp.int32, (P_SIZE, KEEP_MAX), 0)
    row_at = lax.broadcasted_iota(jnp.int32, (P_SIZE, KEEP_MAX), 1)
    hit = (order_ref[:, :KEEP_MAX] == token_at) & (row_at < live)
    return jnp.where(hit, 1.0, 0.0).astype(BF)


def dot(a, b, contract):
    return lax.dot_general(a, b, (((contract[0],), (contract[1],)), ((), ())), preferred_element_type=F32)


def attend_kernel(info, counts, order, query, key, value, mixed, query_c, key_c, value_c, weight, pick):
    live = counts[info[0]]

    @pl.when(pl.program_id(0) == 0)
    def _():
        pick[...] = rows_by_token(order, live)

    tokens = jnp.concatenate([query[0], key[0], value[0]], axis=1)
    rows = dot(pick[...], tokens, (1, 0)).astype(BF)
    q, k, v = rows[:, :128], rows[:, 128:256], rows[:, 256:]
    query_c[...], key_c[...], value_c[...] = q, k, v
    scores = dot(q, k, (1, 1)) * HEAD_DIM ** (-0.5)
    column = lax.broadcasted_iota(jnp.int32, (KEEP_MAX, KEEP_MAX), 1)
    scores = jnp.where(column < live, scores, -1000000000.0)
    exponent = jnp.exp(scores - jnp.max(scores, axis=-1, keepdims=True))
    w = exponent / jnp.sum(exponent, axis=-1, keepdims=True)
    weight[0] = w
    mixed[...] = dot(w.astype(BF), v, (1, 0)).astype(BF)


def attend(info, counts, order, query, key, value):
    heads = query.shape[2] // HEAD_DIM
    token_spec = pl.BlockSpec((1, P_SIZE, HEAD_DIM), lambda h, *_: (0, 0, h))
    row_spec = pl.BlockSpec((KEEP_MAX, HEAD_DIM), lambda h, *_: (0, h))
    row_shape = jax.ShapeDtypeStruct((KEEP_MAX, heads * HEAD_DIM), BF)
    return call(
        attend_kernel, (heads,), (info, counts),
        [pl.BlockSpec((1, P_SIZE), lambda h, *_: (0, 0)), token_spec, token_spec, token_spec],
        [row_spec] * 4 + [pl.BlockSpec((1, KEEP_MAX, KEEP_MAX), lambda h, *_: (h, 0, 0))],
        [row_shape] * 4 + [jax.ShapeDtypeStruct((heads, KEEP_MAX, KEEP_MAX), F32)],
        [pltpu.VMEM((KEEP_MAX, P_SIZE), BF)],
        order, query, key, value,
    )


def attend_back_kernel(info, counts, order, grad, query, key, value, weight, grad_q, grad_k, grad_v, place):
    live = counts[info[0]]

    @pl.when(pl.program_id(0) == 0)
    def _():
        place[...] = tokens_by_row(order, live)

    g, q, k, v = grad[...], query[...], key[...], value[...]
    w = weight[0]
    d_weight = dot(g, v, (1, 1)).astype(BF).astype(F32)
    inner = jnp.sum(d_weight * w, axis=-1, keepdims=True)
    d_scores = (w * (d_weight - inner) * HEAD_DIM ** (-0.5)).astype(BF)
    dq = dot(d_scores, k, (1, 0)).astype(BF)
    dk = dot(d_scores, q, (0, 0)).astype(BF)
    dv = dot(w.astype(BF), g, (0, 0)).astype(BF)
    out = dot(place[...], jnp.concatenate([dq, dk, dv], axis=1), (1, 0)).astype(BF)
    grad_q[0], grad_k[0], grad_v[0] = out[:, :128], out[:, 128:256], out[:, 256:]


def attend_back(info, counts, order, grad, query, key, value, weight):
    heads = query.shape[1] // HEAD_DIM
    token_spec = pl.BlockSpec((1, P_SIZE, HEAD_DIM), lambda h, *_: (0, 0, h))
    row_spec = pl.BlockSpec((KEEP_MAX, HEAD_DIM), lambda h, *_: (0, h))
    token_shape = jax.ShapeDtypeStruct((1, P_SIZE, heads * HEAD_DIM), BF)
    return call(
        attend_back_kernel, (heads,), (info, counts),
        [pl.BlockSpec((1, P_SIZE), lambda h, *_: (0, 0))] + [row_spec] * 4
        + [pl.BlockSpec((1, KEEP_MAX, KEEP_MAX), lambda h, *_: (h, 0, 0))],
        [token_spec] * 3, [token_shape] * 3,
        [pltpu.VMEM((P_SIZE, KEEP_MAX), BF)],
        order, grad, query, key, value, weight,
    )


def pick_kernel(info, counts, order, tokens, rows, pick):
    @pl.when(pl.program_id(0) == 0)
    def _():
        pick[...] = rows_by_token(order, counts[info[0]])

    rows[...] = dot(pick[...], tokens[0], (1, 0)).astype(BF)


def pick_rows(info, counts, order, tokens):
    width = tokens.shape[2]
    return call(
        pick_kernel, (width // 256,), (info, counts),
        [pl.BlockSpec((1, P_SIZE), lambda j, *_: (0, 0)), pl.BlockSpec((1, P_SIZE, 256), lambda j, *_: (0, 0, j))],
        pl.BlockSpec((KEEP_MAX, 256), lambda j, *_: (0, j)),
        jax.ShapeDtypeStruct((KEEP_MAX, width), BF),
        [pltpu.VMEM((KEEP_MAX, P_SIZE), BF)],
        order, tokens,
    )


def place_kernel(info, counts, order, rows, tokens, place):
    @pl.when(pl.program_id(0) == 0)
    def _():
        place[...] = tokens_by_row(order, counts[info[0]])

    tokens[0] = dot(place[...], rows[...], (1, 0)).astype(BF)


def place_rows(info, counts, order, rows):
    width = rows.shape[1]
    return call(
        place_kernel, (width // 256,), (info, counts),
        [pl.BlockSpec((1, P_SIZE), lambda j, *_: (0, 0)), pl.BlockSpec((KEEP_MAX, 256), lambda j, *_: (0, j))],
        pl.BlockSpec((1, P_SIZE, 256), lambda j, *_: (0, 0, j)),
        jax.ShapeDtypeStruct((1, P_SIZE, width), BF),
        [pltpu.VMEM((P_SIZE, KEEP_MAX), BF)],
        order, rows,
    )


def cut_kernel(info, left, right, out):
    ranks, _, width = out.shape
    half = width // 2
    for m in range(ranks):
        out[m, :, :half] = left[:, m * width:m * width + half]
        out[m, :, half:] = right[:, m * width + half:(m + 1) * width]


def assemble_kernel(info, *refs):
    *pieces, out = refs
    _, rows, width = out.shape
    half, part = width // 2, rows // 8
    for stream in range(2):
        for at, step in enumerate(STEPS):
            quarter = lax.rem(info[2 + stream] + 4 + step, 4)
            for core in range(2):
                side = info[4] if core == 0 else 1 - info[4]
                start = pl.multiple_of((side * 4 + quarter) * part, 16)
                piece = pieces[(stream * 4 + at) * 2 + core]
                out[:, pl.ds(start, part), stream * half:(stream + 1) * half] = piece[...]


def gather_columns(info, out_proj, chips):
    rows, full = out_proj.shape
    ranks = lax.axis_size("mp")
    width = full // ranks
    half, part = width // 2, rows // 8
    cut = call(
        cut_kernel, (1,), (info,),
        [
            pl.BlockSpec((part, full), lambda _, i: (i[4] * 4 + i[2], 0)),
            pl.BlockSpec((part, full), lambda _, i: (i[4] * 4 + i[3], 0)),
        ],
        pl.BlockSpec((ranks, part, width), lambda _, i: (0, 0, 0)),
        jax.ShapeDtypeStruct((ranks, part, width), BF), [],
        out_proj, out_proj,
    )
    got = lax.all_to_all(cut, "mp", split_axis=0, concat_axis=0, tiled=True)
    swap = [(dp_index(y, x, c), dp_index(y, x, 1 - c)) for y, x, c in chips]
    pieces = []
    for stream in range(2):
        own = got[:, :, stream * half:(stream + 1) * half]
        for s in STEPS:
            if stream == 0:
                table = [(dp_index(y, x, c), dp_index(y - s, x, c)) for y, x, c in chips]
            else:
                table = [(dp_index(y, x, c), dp_index(y, x - s, c)) for y, x, c in chips]
            piece = own if s == 0 else lax.ppermute(own, "dp", table)
            pieces += [piece, lax.ppermute(piece, "dp", swap)]
    steps = 2
    whole = call(
        assemble_kernel, (steps,), (info,),
        [pl.BlockSpec((ranks // steps, part, half), lambda m, i: (m, 0, 0))] * 16,
        pl.BlockSpec((ranks // steps, rows, width), lambda m, i: (m, 0, 0)),
        jax.ShapeDtypeStruct((ranks, rows, width), BF), [],
        *pieces,
    )
    return cut, whole.reshape(ranks * rows, width)


def project_kernel(info, mixed, weight, grad, gain, projected, sums):
    step = pl.program_id(0)
    part = dot(mixed[...], weight[...], (1, 0))

    @pl.when(step == 0)
    def _():
        projected[...] = part

    @pl.when(step > 0)
    def _():
        projected[...] += part

    @pl.when(step == pl.num_programs(0) - 1)
    def _():
        values = projected[...]
        scaled = grad[...].astype(F32) * gain[...].astype(F32)
        lane = lax.broadcasted_iota(jnp.int32, (KEEP_MAX, 128), 1)
        table = jnp.zeros((KEEP_MAX, 128), F32)
        for at, term in enumerate((values, values * values, scaled, scaled * values)):
            table = jnp.where(lane == at, jnp.sum(term, axis=-1, keepdims=True), table)
        sums[...] = jnp.transpose(table)[:8]


def project(info, mixed, weight, grad, gain):
    depth, width = weight.shape
    block = 768
    return call(
        project_kernel, (depth // block,), (info,),
        [
            pl.BlockSpec((KEEP_MAX, block), lambda k, i: (0, k)),
            pl.BlockSpec((block, width), lambda k, i: (k, 0)),
            pl.BlockSpec((KEEP_MAX, width), lambda k, i: (0, 0)),
            pl.BlockSpec((1, width), lambda k, i: (0, i[1])),
        ],
        [pl.BlockSpec((KEEP_MAX, width), lambda k, i: (0, 0)), pl.BlockSpec((8, KEEP_MAX), lambda k, i: (0, 0))],
        [jax.ShapeDtypeStruct((KEEP_MAX, width), F32), jax.ShapeDtypeStruct((8, KEEP_MAX), F32)],
        [], mixed, weight, grad, gain,
    )


def grad_kernel(full_width, info, counts, projected, grad, gain, weight, *refs):
    *sums, out, grad_proj, normed = refs

    @pl.when(pl.program_id(0) == 0)
    def _():
        total = sums[0][...]
        for other in sums[1:]:
            total = total + other[...]
        total = jnp.concatenate([total, jnp.zeros((120, KEEP_MAX), F32)], axis=0)
        table = jnp.transpose(total) / full_width
        row_mean, row_square, first, cross = (table[:, at:at + 1] for at in range(4))
        inv_std = lax.rsqrt(row_square - row_mean * row_mean + 1e-06)
        second = (cross - row_mean * first) * inv_std
        live = lax.broadcasted_iota(jnp.int32, (KEEP_MAX, 1), 0) < counts[info[0]]
        gain_wide = gain[...].astype(F32)
        centred = (projected[...] - row_mean) * inv_std
        scaled = grad[...].astype(F32) * gain_wide
        normed[...] = jnp.where(live, centred * gain_wide, 0.0).astype(BF)
        grad_proj[...] = jnp.where(live, inv_std * (scaled - first - centred * second), 0.0).astype(BF)

    product = dot(grad_proj[...], weight[...], (1, 1)).astype(BF)
    half = out.shape[2]
    out[0] = product[:, :half]
    out[1] = product[:, half:]


def grad_rows(info, counts, projected, grad, gain, weight, sums, full_width):
    depth, width = weight.shape
    block = 768
    whole = pl.BlockSpec((KEEP_MAX, width), lambda k, *i: (0, 0))
    rows_shape = jax.ShapeDtypeStruct((KEEP_MAX, width), BF)
    return call(
        functools.partial(grad_kernel, full_width), (depth // block,), (info, counts),
        [
            whole, whole,
            pl.BlockSpec((1, width), lambda k, i, c: (0, i[1])),
            pl.BlockSpec((block, width), lambda k, *i: (k, 0)),
        ] + [pl.BlockSpec((8, KEEP_MAX), lambda k, *i: (0, 0))] * len(sums),
        [pl.BlockSpec((2, KEEP_MAX, block // 2), lambda k, *i: (k, 0, 0)), whole, whole],
        [jax.ShapeDtypeStruct((depth * 2 // block, KEEP_MAX, block // 2), BF), rows_shape, rows_shape],
        [], projected, grad, gain, weight, *sums,
    )


def outer_kernel(info, own_grad, other_grad, own_mixed, other_mixed, out, turned):
    @pl.when(pl.program_id(0) == 0)
    def _():
        turned[:, :KEEP_MAX] = jnp.transpose(own_grad[...])
        turned[:, KEEP_MAX:] = jnp.transpose(other_grad[...])

    rows = jnp.concatenate([own_mixed[...], other_mixed[...]], axis=0)
    out[0] = dot(turned[...], rows, (1, 0)).astype(BF)


def outer(info, own_grad, other_grad, mixed, other_mixed):
    width = own_grad.shape[1]
    block = mixed.shape[1] // 8
    grad_spec = pl.BlockSpec((KEEP_MAX, width), lambda j, i: (0, 0))
    return call(
        outer_kernel, (4,), (info,),
        [
            grad_spec, grad_spec,
            pl.BlockSpec((KEEP_MAX, block), lambda j, i: (0, i[4] * 4 + j)),
            pl.BlockSpec((KEEP_MAX, block), lambda j, i: (0, i[4] * 4 + j)),
        ],
        pl.BlockSpec((1, width, block), lambda j, i: (j, 0, 0)),
        jax.ShapeDtypeStruct((4, width, block), BF),
        [pltpu.VMEM((width, 2 * KEEP_MAX), BF)],
        own_grad, other_grad, mixed, other_mixed,
    )


def dp_index(y, x, core):
    return (y % 4) * 8 + (x % 4) * 2 + core


def on_device(
    query_heads, key_heads, value_heads, out_proj, norm_gain, keep_order, keep_count, cotangent
):
    ranks = lax.axis_size("mp")
    image = lax.axis_index("dp")
    rank = lax.axis_index("mp")
    info = jnp.stack([image, rank, image // 8, (image // 2) % 4, image % 2]).astype(jnp.int32)
    chips = [(y, x, core) for y in range(4) for x in range(4) for core in range(2)]
    swap = [(dp_index(y, x, c), dp_index(y, x, 1 - c)) for y, x, c in chips]
    gain = norm_gain.reshape(1, -1)

    cut, columns = gather_columns(info, out_proj, chips)
    early, _ = lax.optimization_barrier((info, cut))
    mixed, query_c, key_c, value_c, weights = attend(
        early, keep_count, keep_order, query_heads, key_heads, value_heads
    )
    mixed_all = lax.all_gather(mixed, "mp", axis=1, tiled=True)
    late, _ = lax.optimization_barrier((info, columns))
    grad_c = pick_rows(late, keep_count, keep_order, cotangent)
    mixed_all, columns, grad_c = lax.optimization_barrier((mixed_all, columns, grad_c))
    projected, sums = project(info, mixed_all, columns, grad_c, gain)
    pair_sums = sums + lax.ppermute(sums, "mp", [(m, m ^ 1) for m in range(ranks)])
    all_sums = [pair_sums] + [
        lax.ppermute(pair_sums, "mp", [(m, m ^ s) for m in range(ranks)]) for s in range(2, ranks, 2)
    ]
    other_mixed = lax.ppermute(mixed_all, "dp", swap)
    all_sums, other_mixed = lax.optimization_barrier((all_sums, other_mixed))
    mixed_grad, grad_proj, normed_c = grad_rows(
        info, keep_count, projected, grad_c, gain, columns, all_sums, norm_gain.shape[0]
    )
    grad_mixed = lax.psum_scatter(mixed_grad, "mp", scatter_dimension=0, tiled=True)[0]

    other_grad = lax.ppermute(grad_proj, "dp", swap)
    normed = place_rows(info, keep_count, keep_order, normed_c)
    pair = outer(info, grad_proj, other_grad, mixed_all, other_mixed)
    width, depth = pair.shape[1], pair.shape[2]
    pair = pair.reshape(16, width // 4, depth)
    groups = [[2 * j + c for j in range(16)] for c in range(2)]
    spread = lax.all_to_all(
        pair, "dp", split_axis=0, concat_axis=0, tiled=True, axis_index_groups=groups
    )
    total = jnp.sum(spread.astype(F32), axis=0).astype(BF)
    home = [
        (dp_index(y, x, c) * ranks + m, (4 * m + x) * ranks + 4 * c + y)
        for y, x, c in chips for m in range(ranks)
    ]
    total = lax.ppermute(total, ("dp", "mp"), home)

    grads = attend_back(info, keep_count, keep_order, grad_mixed, query_c, key_c, value_c, weights)
    total, grads, normed = lax.optimization_barrier((total, grads, normed))
    return (normed, *grads, total.astype(F32).T)


def solution(mesh):
    in_specs = (
        P("dp", None, "mp"),
        P("dp", None, "mp"),
        P("dp", None, "mp"),
        P("mp", None),
        P(),
        P("dp", None),
        P(),
        P("dp", None, "mp"),
    )
    out_specs = (
        P("dp", None, "mp"),
        P("dp", None, "mp"),
        P("dp", None, "mp"),
        P("dp", None, "mp"),
        P("mp", "dp"),
    )
    return jax.shard_map(
        on_device, mesh=mesh, in_specs=in_specs, out_specs=out_specs, check_vma=False
    )
```

```python
import functools

import jax
import jax.numpy as jnp
from jax import lax
from jax.experimental import pallas as pl
from jax.experimental.pallas import tpu as pltpu
from jax.sharding import PartitionSpec as P

HEAD_DIM = 128
P_SIZE = 1024
KEEP_MAX = 512
MIB = 1024 * 1024
BF = jnp.bfloat16
F32 = jnp.float32
STEPS = (0, -1, 1, 2)


def call(kernel, grid, prefetched, in_specs, out_specs, out_shape, scratch, *operands, vmem):
    moved = 2 * sum(a.size * a.dtype.itemsize for a in operands)
    return pl.pallas_call(
        kernel,
        grid_spec=pltpu.PrefetchScalarGridSpec(
            num_scalar_prefetch=len(prefetched),
            grid=grid,
            in_specs=in_specs,
            out_specs=out_specs,
            scratch_shapes=scratch,
        ),
        out_shape=out_shape,
        compiler_params=pltpu.CompilerParams(vmem_limit_bytes=vmem * MIB),
        cost_estimate=pl.CostEstimate(flops=0, bytes_accessed=moved, transcendentals=0),
    )(*prefetched, *operands)


def in_hbm(x):
    return pltpu.with_memory_space_constraint(x, pltpu.HBM)


def in_vmem(x):
    return pltpu.with_memory_space_constraint(x, pltpu.VMEM)


def to_column(row):
    wide = jnp.broadcast_to(row, (128, row.shape[1]))
    return jnp.transpose(wide)[:, :1]


def rows_by_token(order_ref, live):
    token = to_column(order_ref[:, :KEEP_MAX].astype(F32)).astype(jnp.int32)
    row_at = lax.broadcasted_iota(jnp.int32, (KEEP_MAX, P_SIZE), 0)
    token_at = lax.broadcasted_iota(jnp.int32, (KEEP_MAX, P_SIZE), 1)
    return jnp.where((token == token_at) & (row_at < live), 1.0, 0.0).astype(BF)


def tokens_by_row(order_ref, live):
    token_at = lax.broadcasted_iota(jnp.int32, (P_SIZE, KEEP_MAX), 0)
    row_at = lax.broadcasted_iota(jnp.int32, (P_SIZE, KEEP_MAX), 1)
    hit = (order_ref[:, :KEEP_MAX] == token_at) & (row_at < live)
    return jnp.where(hit, 1.0, 0.0).astype(BF)


def dot(a, b, contract):
    return lax.dot_general(a, b, (((contract[0],), (contract[1],)), ((), ())), preferred_element_type=F32)


def attend_kernel(info, counts, order, query, key, value, mixed, query_c, key_c, value_c, weight, pick):
    live = counts[info[0]]

    @pl.when(pl.program_id(0) == 0)
    def _():
        pick[...] = rows_by_token(order, live)

    tokens = jnp.concatenate([query[0], key[0], value[0]], axis=1)
    rows = dot(pick[...], tokens, (1, 0)).astype(BF)
    q, k, v = rows[:, :128], rows[:, 128:256], rows[:, 256:]
    query_c[...], key_c[...], value_c[...] = q, k, v
    scores = dot(q, k, (1, 1)) * HEAD_DIM ** (-0.5)
    column = lax.broadcasted_iota(jnp.int32, (KEEP_MAX, KEEP_MAX), 1)
    scores = jnp.where(column < live, scores, -1000000000.0)
    exponent = jnp.exp(scores - jnp.max(scores, axis=-1, keepdims=True))
    w = exponent / jnp.sum(exponent, axis=-1, keepdims=True)
    weight[0] = w
    mixed[...] = dot(w.astype(BF), v, (1, 0)).astype(BF)


def attend(info, counts, order, query, key, value):
    heads = query.shape[2] // HEAD_DIM
    token_spec = pl.BlockSpec((1, P_SIZE, HEAD_DIM), lambda h, *_: (0, 0, h))
    row_spec = pl.BlockSpec((KEEP_MAX, HEAD_DIM), lambda h, *_: (0, h))
    row_shape = pltpu.HBM((KEEP_MAX, heads * HEAD_DIM), BF)
    return call(
        attend_kernel, (heads,), (info, counts),
        [pl.BlockSpec((1, P_SIZE), lambda h, *_: (0, 0)), token_spec, token_spec, token_spec],
        [row_spec] * 4 + [pl.BlockSpec((1, KEEP_MAX, KEEP_MAX), lambda h, *_: (h, 0, 0))],
        [row_shape] * 4 + [pltpu.HBM((heads, KEEP_MAX, KEEP_MAX), F32)],
        [pltpu.VMEM((KEEP_MAX, P_SIZE), BF)],
        in_hbm(order), in_hbm(query), in_hbm(key), in_hbm(value), vmem=20,
    )


def attend_back_kernel(info, counts, order, grad, query, key, value, weight, grad_q, grad_k, grad_v, place):
    live = counts[info[0]]

    @pl.when(pl.program_id(0) == 0)
    def _():
        place[...] = tokens_by_row(order, live)

    g, q, k, v = grad[...], query[...], key[...], value[...]
    w = weight[0]
    d_weight = dot(g, v, (1, 1)).astype(BF).astype(F32)
    inner = jnp.sum(d_weight * w, axis=-1, keepdims=True)
    d_scores = (w * (d_weight - inner) * HEAD_DIM ** (-0.5)).astype(BF)
    dq = dot(d_scores, k, (1, 0)).astype(BF)
    dk = dot(d_scores, q, (0, 0)).astype(BF)
    dv = dot(w.astype(BF), g, (0, 0)).astype(BF)
    out = dot(place[...], jnp.concatenate([dq, dk, dv], axis=1), (1, 0)).astype(BF)
    grad_q[0], grad_k[0], grad_v[0] = out[:, :128], out[:, 128:256], out[:, 256:]


def attend_back(info, counts, order, grad, query, key, value, weight):
    heads = query.shape[1] // HEAD_DIM
    token_spec = pl.BlockSpec((1, P_SIZE, HEAD_DIM), lambda h, *_: (0, 0, h))
    row_spec = pl.BlockSpec((KEEP_MAX, HEAD_DIM), lambda h, *_: (0, h))
    token_shape = jax.ShapeDtypeStruct((1, P_SIZE, heads * HEAD_DIM), BF)
    return call(
        attend_back_kernel, (heads,), (info, counts),
        [pl.BlockSpec((1, P_SIZE), lambda h, *_: (0, 0))] + [row_spec] * 4
        + [pl.BlockSpec((1, KEEP_MAX, KEEP_MAX), lambda h, *_: (h, 0, 0))],
        [token_spec] * 3, [token_shape] * 3,
        [pltpu.VMEM((P_SIZE, KEEP_MAX), BF)],
        in_hbm(order), in_hbm(grad), in_hbm(query), in_hbm(key), in_hbm(value), in_hbm(weight), vmem=20,
    )


def pick_kernel(info, counts, order, tokens, rows, pick):
    @pl.when(pl.program_id(0) == 0)
    def _():
        pick[...] = rows_by_token(order, counts[info[0]])

    rows[...] = dot(pick[...], tokens[0], (1, 0)).astype(BF)


def pick_rows(info, counts, order, tokens):
    width = tokens.shape[2]
    return call(
        pick_kernel, (width // 256,), (info, counts),
        [pl.BlockSpec((1, P_SIZE), lambda j, *_: (0, 0)), pl.BlockSpec((1, P_SIZE, 256), lambda j, *_: (0, 0, j))],
        pl.BlockSpec((KEEP_MAX, 256), lambda j, *_: (0, j)),
        jax.ShapeDtypeStruct((KEEP_MAX, width), BF),
        [pltpu.VMEM((KEEP_MAX, P_SIZE), BF)],
        order, tokens, vmem=12,
    )


def place_kernel(info, counts, order, rows, tokens, place):
    @pl.when(pl.program_id(0) == 0)
    def _():
        place[...] = tokens_by_row(order, counts[info[0]])

    tokens[0] = dot(place[...], rows[...], (1, 0)).astype(BF)


def place_rows(info, counts, order, rows):
    width = rows.shape[1]
    return call(
        place_kernel, (width // 256,), (info, counts),
        [pl.BlockSpec((1, P_SIZE), lambda j, *_: (0, 0)), pl.BlockSpec((KEEP_MAX, 256), lambda j, *_: (0, j))],
        pl.BlockSpec((1, P_SIZE, 256), lambda j, *_: (0, 0, j)),
        jax.ShapeDtypeStruct((1, P_SIZE, width), BF),
        [pltpu.VMEM((P_SIZE, KEEP_MAX), BF)],
        order, in_hbm(rows), vmem=12,
    )


def shift_of(y, core):
    return y if core == 0 else (8 - y if y else 4)


def cut_kernel(info, block, out):
    half = out.shape[2]
    out[0] = block[:, :half]
    out[1] = block[:, half:]


def fetch_columns(info, out_proj, chips):
    rows, full = out_proj.shape
    ranks = lax.axis_size("mp")
    width, part = full // ranks, rows // 4
    half = width // 2
    parts = call(
        cut_kernel, (1,), (info,),
        [pl.BlockSpec((part, width), lambda _, i: (i[3], lax.rem(i[1] + ranks - i[5], ranks)))],
        pl.BlockSpec((2, part, half), lambda _, i: (0, 0, 0)),
        jax.ShapeDtypeStruct((2, part, half), BF), [],
        in_hbm(out_proj), vmem=4,
    )
    table = [
        (dp_index(y, x, c) * ranks + m, dp_index(y, x, c) * ranks + (m - shift_of(y, c)) % ranks)
        for y, x, c in chips for m in range(ranks)
    ]
    got = lax.ppermute(parts, ("dp", "mp"), table)
    return got[0], got[1]


def spread_columns(parts, chips, after, beside):
    swap = [(dp_index(y, x, c), dp_index(y, x, 1 - c)) for y, x, c in chips]
    along = {
        "y": {s: [(dp_index(y, x, c), dp_index(y - s, x, c)) for y, x, c in chips] for s in STEPS[1:]},
        "x": {s: [(dp_index(y, x, c), dp_index(y, x - s, c)) for y, x, c in chips] for s in STEPS[1:]},
    }
    ways = (("y", "x"), ("x", "y"))
    first = [
        [part] + [lax.ppermute(part, "dp", along[way][s]) for s in STEPS[1:]]
        for part, (way, _) in zip(parts, ways)
    ]
    fours = [jnp.stack(pieces) for pieces in first]
    after, fours = lax.optimization_barrier((after, fours))
    done = beside(after)
    pieces = []
    for four, (_, way) in zip(fours, ways):
        for s in STEPS:
            piece = four if s == 0 else lax.ppermute(four, "dp", along[way][s])
            if way == "y" and s == STEPS[-1]:
                piece, *done = lax.optimization_barrier((piece, *done))
            pieces += [piece, lax.ppermute(piece, "dp", swap)]
    return pieces, done


def assemble_kernel(info, *refs):
    *pieces, out = refs
    ranks, rows, width = out.shape
    half, part = width // 2, rows // 4
    for stream in range(2):
        for at, second in enumerate(STEPS):
            for core in range(2):
                piece = pieces[(stream * 4 + at) * 2 + core]
                side = info[4] if core == 0 else 1 - info[4]
                for j, first in enumerate(STEPS):
                    dy, dx = (first, second) if stream == 0 else (second, first)
                    y, x = lax.rem(info[2] + 4 + dy, 4), lax.rem(info[3] + 4 + dx, 4)
                    shift = jnp.where(side == 0, y, jnp.where(y == 0, 4, 8 - y))
                    start = pl.multiple_of(x * part, 16)
                    out[lax.rem(info[1] + shift, ranks), pl.ds(start, part), stream * half:(stream + 1) * half] = piece[j]


def assemble(info, pieces, ranks):
    four, part, half = pieces[0].shape
    rows, width = four * part, 2 * half
    whole = call(
        assemble_kernel, (1,), (info,),
        [pl.BlockSpec((four, part, half), lambda _, i: (0, 0, 0))] * 16,
        pl.BlockSpec((ranks, rows, width), lambda _, i: (0, 0, 0)),
        pltpu.HBM((ranks, rows, width), BF), [],
        *pieces, vmem=24,
    )
    return whole.reshape(ranks * rows, width)


def project_kernel(info, mixed, weight, grad, gain, projected, sums):
    step = pl.program_id(0)
    part = dot(mixed[...], weight[...], (1, 0))

    @pl.when(step == 0)
    def _():
        projected[...] = part

    @pl.when(step > 0)
    def _():
        projected[...] += part

    @pl.when(step == pl.num_programs(0) - 1)
    def _():
        values = projected[...]
        scaled = grad[...].astype(F32) * gain[...].astype(F32)
        lane = lax.broadcasted_iota(jnp.int32, (KEEP_MAX, 128), 1)
        table = jnp.zeros((KEEP_MAX, 128), F32)
        for at, term in enumerate((values, values * values, scaled, scaled * values)):
            table = jnp.where(lane == at, jnp.sum(term, axis=-1, keepdims=True), table)
        sums[...] = jnp.transpose(table)[:8]


def project(info, mixed, weight, grad, gain):
    depth, width = weight.shape
    block = 768
    return call(
        project_kernel, (depth // block,), (info,),
        [
            pl.BlockSpec((KEEP_MAX, block), lambda k, i: (0, k)),
            pl.BlockSpec((block, width), lambda k, i: (k, 0)),
            pl.BlockSpec((KEEP_MAX, width), lambda k, i: (0, 0)),
            pl.BlockSpec((1, width), lambda k, i: (0, i[1])),
        ],
        [pl.BlockSpec((KEEP_MAX, width), lambda k, i: (0, 0)), pl.BlockSpec((8, KEEP_MAX), lambda k, i: (0, 0))],
        [jax.ShapeDtypeStruct((KEEP_MAX, width), F32), jax.ShapeDtypeStruct((8, KEEP_MAX), F32)],
        [], in_hbm(mixed), in_hbm(weight), grad, gain, vmem=18,
    )


def grad_kernel(full_width, info, counts, projected, grad, gain, *refs):
    *sums, grad_proj, normed = refs
    total = sums[0][...]
    for other in sums[1:]:
        total = total + other[...]
    total = jnp.concatenate([total, jnp.zeros((120, KEEP_MAX), F32)], axis=0)
    table = jnp.transpose(total) / full_width
    row_mean, row_square, first, cross = (table[:, at:at + 1] for at in range(4))
    inv_std = lax.rsqrt(row_square - row_mean * row_mean + 1e-06)
    second = (cross - row_mean * first) * inv_std
    live = lax.broadcasted_iota(jnp.int32, (KEEP_MAX, 1), 0) < counts[info[0]]
    gain_wide = gain[...].astype(F32)
    centred = (projected[...] - row_mean) * inv_std
    scaled = grad[...].astype(F32) * gain_wide
    normed[...] = jnp.where(live, centred * gain_wide, 0.0).astype(BF)
    grad_proj[...] = jnp.where(live, inv_std * (scaled - first - centred * second), 0.0).astype(BF)


def grad_rows(info, counts, projected, grad, gain, sums, full_width):
    width = projected.shape[1]
    whole = pl.BlockSpec((KEEP_MAX, width), lambda k, *i: (0, 0))
    shape = (KEEP_MAX, width)
    return call(
        functools.partial(grad_kernel, full_width), (1,), (info, counts),
        [whole, whole, pl.BlockSpec((1, width), lambda k, i, c: (0, i[1]))]
        + [pl.BlockSpec((8, KEEP_MAX), lambda k, *i: (0, 0))] * len(sums),
        [whole, whole], [pltpu.VMEM(shape, BF), pltpu.HBM(shape, BF)],
        [], projected, grad, gain, *sums, vmem=20,
    )


def back_kernel(grad_proj, weight, out):
    product = dot(grad_proj[...], weight[...], (1, 1)).astype(BF)
    half = out.shape[2]
    out[0] = product[:, :half]
    out[1] = product[:, half:]


def project_back(grad_proj, weight):
    depth, width = weight.shape
    block = 768
    return call(
        back_kernel, (depth // block,), (),
        [pl.BlockSpec((KEEP_MAX, width), lambda k: (0, 0)), pl.BlockSpec((block, width), lambda k: (k, 0))],
        pl.BlockSpec((2, KEEP_MAX, block // 2), lambda k: (k, 0, 0)),
        pltpu.HBM((depth * 2 // block, KEEP_MAX, block // 2), BF),
        [], grad_proj, in_vmem(weight), vmem=12,
    )


def outer_kernel(info, own_grad, other_grad, own_mixed, other_mixed, out, turned):
    @pl.when(pl.program_id(0) == 0)
    def _():
        turned[:, :KEEP_MAX] = jnp.transpose(own_grad[...])
        turned[:, KEEP_MAX:] = jnp.transpose(other_grad[...])

    rows = jnp.concatenate([own_mixed[...], other_mixed[...]], axis=0)
    out[0] = dot(turned[...], rows, (1, 0)).astype(BF)


def outer(info, own_grad, other_grad, mixed, other_mixed):
    width = own_grad.shape[1]
    block = mixed.shape[1] // 8
    grad_spec = pl.BlockSpec((KEEP_MAX, width), lambda j, i: (0, 0))
    return call(
        outer_kernel, (4,), (info,),
        [
            grad_spec, grad_spec,
            pl.BlockSpec((KEEP_MAX, block), lambda j, i: (0, i[4] * 4 + j)),
            pl.BlockSpec((KEEP_MAX, block), lambda j, i: (0, i[4] * 4 + j)),
        ],
        pl.BlockSpec((1, width, block), lambda j, i: (j, 0, 0)),
        jax.ShapeDtypeStruct((4, width, block), BF),
        [pltpu.VMEM((width, 2 * KEEP_MAX), BF)],
        own_grad, other_grad, in_hbm(mixed), in_hbm(other_mixed), vmem=16,
    )


def dp_index(y, x, core):
    return (y % 4) * 8 + (x % 4) * 2 + core


def on_device(
    query_heads, key_heads, value_heads, out_proj, norm_gain, keep_order, keep_count, cotangent
):
    ranks = lax.axis_size("mp")
    image = lax.axis_index("dp")
    rank = lax.axis_index("mp")
    y_at, core = image // 8, image % 2
    shift = jnp.where(core == 0, y_at, jnp.where(y_at == 0, 4, 8 - y_at))
    info = jnp.stack([image, rank, y_at, (image // 2) % 4, core, shift]).astype(jnp.int32)
    chips = [(y, x, core) for y in range(4) for x in range(4) for core in range(2)]
    swap = [(dp_index(y, x, c), dp_index(y, x, 1 - c)) for y, x, c in chips]

    mixed, query_c, key_c, value_c, weights = attend(
        info, keep_count, keep_order, query_heads, key_heads, value_heads
    )
    later, mixed = lax.optimization_barrier((info, mixed))
    parts = fetch_columns(later, out_proj, chips)
    mixed_all = lax.all_gather(mixed, "mp", axis=1, tiled=True)
    pieces, (grad_c, gain) = spread_columns(
        parts, chips, info,
        lambda after: (pick_rows(after, keep_count, keep_order, cotangent), norm_gain.reshape(1, -1)),
    )
    columns = assemble(info, pieces, ranks)
    mixed_all, grad_c, columns = lax.optimization_barrier((mixed_all, grad_c, columns))
    projected, sums = project(info, mixed_all, columns, grad_c, gain)
    pair_sums = sums + lax.ppermute(sums, "mp", [(m, m ^ 1) for m in range(ranks)])
    all_sums = [pair_sums] + [
        lax.ppermute(pair_sums, "mp", [(m, m ^ s) for m in range(ranks)]) for s in range(2, ranks, 2)
    ]
    other_mixed = lax.ppermute(mixed_all, "dp", swap)
    all_sums, other_mixed = lax.optimization_barrier((all_sums, other_mixed))
    grad_proj, normed_c = grad_rows(
        info, keep_count, projected, grad_c, gain, all_sums, norm_gain.shape[0]
    )
    mixed_grad = project_back(grad_proj, columns)
    other_grad = lax.ppermute(grad_proj, "dp", swap)
    mixed_grad, other_grad = lax.optimization_barrier((mixed_grad, other_grad))
    grad_mixed = lax.psum_scatter(mixed_grad, "mp", scatter_dimension=0, tiled=True)[0]

    normed = place_rows(info, keep_count, keep_order, normed_c)
    pair = outer(info, grad_proj, other_grad, mixed_all, other_mixed)
    width, depth = pair.shape[1], pair.shape[2]
    pair = pair.reshape(16, width // 4, depth)
    groups = [[2 * j + c for j in range(16)] for c in range(2)]
    spread = lax.all_to_all(
        pair, "dp", split_axis=0, concat_axis=0, tiled=True, axis_index_groups=groups
    )
    total = jnp.sum(spread.astype(F32), axis=0).astype(BF)
    home = [
        (dp_index(y, x, c) * ranks + m, (4 * m + x) * ranks + 4 * c + y)
        for y, x, c in chips for m in range(ranks)
    ]
    total = lax.ppermute(total, ("dp", "mp"), home)

    grads = attend_back(info, keep_count, keep_order, grad_mixed, query_c, key_c, value_c, weights)
    total, grads, normed = lax.optimization_barrier((total, grads, normed))
    return (normed, *grads, total.astype(F32).T)


def solution(mesh):
    in_specs = (
        P("dp", None, "mp"),
        P("dp", None, "mp"),
        P("dp", None, "mp"),
        P("mp", None),
        P(),
        P("dp", None),
        P(),
        P("dp", None, "mp"),
    )
    out_specs = (
        P("dp", None, "mp"),
        P("dp", None, "mp"),
        P("dp", None, "mp"),
        P("dp", None, "mp"),
        P("mp", "dp"),
    )
    return jax.shard_map(
        on_device, mesh=mesh, in_specs=in_specs, out_specs=out_specs, check_vma=False
    )
```

```python
import functools

import jax
import jax.numpy as jnp
from jax import lax
from jax.experimental import pallas as pl
from jax.experimental.pallas import tpu as pltpu
from jax.sharding import PartitionSpec as P

HEAD_DIM = 128
P_SIZE = 1024
KEEP_MAX = 512
MIB = 1024 * 1024
BF = jnp.bfloat16
F32 = jnp.float32
STEPS = (0, -1, 1, 2)


def call(kernel, grid, prefetched, in_specs, out_specs, out_shape, scratch, *operands, vmem):
    moved = 2 * sum(a.size * a.dtype.itemsize for a in operands)
    return pl.pallas_call(
        kernel,
        grid_spec=pltpu.PrefetchScalarGridSpec(
            num_scalar_prefetch=len(prefetched),
            grid=grid,
            in_specs=in_specs,
            out_specs=out_specs,
            scratch_shapes=scratch,
        ),
        out_shape=out_shape,
        compiler_params=pltpu.CompilerParams(vmem_limit_bytes=vmem * MIB),
        cost_estimate=pl.CostEstimate(flops=0, bytes_accessed=moved, transcendentals=0),
    )(*prefetched, *operands)


def in_hbm(x):
    return pltpu.with_memory_space_constraint(x, pltpu.HBM)


def in_vmem(x):
    return pltpu.with_memory_space_constraint(x, pltpu.VMEM)


def to_column(row):
    wide = jnp.broadcast_to(row, (128, row.shape[1]))
    return jnp.transpose(wide)[:, :1]


def rows_by_token(order_ref, live):
    token = to_column(order_ref[:, :KEEP_MAX].astype(F32)).astype(jnp.int32)
    row_at = lax.broadcasted_iota(jnp.int32, (KEEP_MAX, P_SIZE), 0)
    token_at = lax.broadcasted_iota(jnp.int32, (KEEP_MAX, P_SIZE), 1)
    return jnp.where((token == token_at) & (row_at < live), 1.0, 0.0).astype(BF)


def tokens_by_row(order_ref, live):
    token_at = lax.broadcasted_iota(jnp.int32, (P_SIZE, KEEP_MAX), 0)
    row_at = lax.broadcasted_iota(jnp.int32, (P_SIZE, KEEP_MAX), 1)
    hit = (order_ref[:, :KEEP_MAX] == token_at) & (row_at < live)
    return jnp.where(hit, 1.0, 0.0).astype(BF)


def dot(a, b, contract):
    return lax.dot_general(a, b, (((contract[0],), (contract[1],)), ((), ())), preferred_element_type=F32)


def attend_kernel(info, counts, order, query, key, value, mixed, query_c, key_c, value_c, weight, pick):
    live = counts[info[0]]

    @pl.when(pl.program_id(0) == 0)
    def _():
        pick[...] = rows_by_token(order, live)

    tokens = jnp.concatenate([query[0], key[0], value[0]], axis=1)
    rows = dot(pick[...], tokens, (1, 0)).astype(BF)
    q, k, v = rows[:, :128], rows[:, 128:256], rows[:, 256:]
    query_c[...], key_c[...], value_c[...] = q, k, v
    scores = dot(q, k, (1, 1)) * HEAD_DIM ** (-0.5)
    column = lax.broadcasted_iota(jnp.int32, (KEEP_MAX, KEEP_MAX), 1)
    scores = jnp.where(column < live, scores, -1000000000.0)
    exponent = jnp.exp(scores - jnp.max(scores, axis=-1, keepdims=True))
    w = exponent / jnp.sum(exponent, axis=-1, keepdims=True)
    weight[0] = w
    mixed[...] = dot(w.astype(BF), v, (1, 0)).astype(BF)


def attend(info, counts, order, query, key, value):
    heads = query.shape[2] // HEAD_DIM
    token_spec = pl.BlockSpec((1, P_SIZE, HEAD_DIM), lambda h, *_: (0, 0, h))
    row_spec = pl.BlockSpec((KEEP_MAX, HEAD_DIM), lambda h, *_: (0, h))
    row_shape = pltpu.HBM((KEEP_MAX, heads * HEAD_DIM), BF)
    return call(
        attend_kernel, (heads,), (info, counts),
        [pl.BlockSpec((1, P_SIZE), lambda h, *_: (0, 0)), token_spec, token_spec, token_spec],
        [row_spec] * 4 + [pl.BlockSpec((1, KEEP_MAX, KEEP_MAX), lambda h, *_: (h, 0, 0))],
        [row_shape] * 4 + [pltpu.HBM((heads, KEEP_MAX, KEEP_MAX), F32)],
        [pltpu.VMEM((KEEP_MAX, P_SIZE), BF)],
        in_hbm(order), in_hbm(query), in_hbm(key), in_hbm(value), vmem=20,
    )


def attend_back_kernel(
    info, counts, order, grad, query, key, value, weight, normed, grad_q, grad_k, grad_v, normed_out, place
):
    live = counts[info[0]]

    @pl.when(pl.program_id(0) == 0)
    def _():
        place[...] = tokens_by_row(order, live)

    g, q, k, v = grad[...], query[...], key[...], value[...]
    w = weight[0]
    d_weight = dot(g, v, (1, 1)).astype(BF).astype(F32)
    inner = jnp.sum(d_weight * w, axis=-1, keepdims=True)
    d_scores = (w * (d_weight - inner) * HEAD_DIM ** (-0.5)).astype(BF)
    dq = dot(d_scores, k, (1, 0)).astype(BF)
    dk = dot(d_scores, q, (0, 0)).astype(BF)
    dv = dot(w.astype(BF), g, (0, 0)).astype(BF)
    rows = jnp.concatenate([dq, dk, dv, normed[...]], axis=1)
    out = dot(place[...], rows, (1, 0)).astype(BF)
    grad_q[0], grad_k[0], grad_v[0] = out[:, :128], out[:, 128:256], out[:, 256:384]
    normed_out[0] = out[:, 384:]


def attend_back(info, counts, order, grad, query, key, value, weight, normed):
    heads = query.shape[1] // HEAD_DIM
    width = normed.shape[1]
    token_spec = pl.BlockSpec((1, P_SIZE, HEAD_DIM), lambda h, *_: (0, 0, h))
    row_spec = pl.BlockSpec((KEEP_MAX, HEAD_DIM), lambda h, *_: (0, h))
    token_shape = jax.ShapeDtypeStruct((1, P_SIZE, heads * HEAD_DIM), BF)
    return call(
        attend_back_kernel, (heads,), (info, counts),
        [pl.BlockSpec((1, P_SIZE), lambda h, *_: (0, 0))] + [row_spec] * 4
        + [pl.BlockSpec((1, KEEP_MAX, KEEP_MAX), lambda h, *_: (h, 0, 0)),
           pl.BlockSpec((KEEP_MAX, width // heads), lambda h, *_: (0, h))],
        [token_spec] * 3 + [pl.BlockSpec((1, P_SIZE, width // heads), lambda h, *_: (0, 0, h))],
        [token_shape] * 3 + [jax.ShapeDtypeStruct((1, P_SIZE, width), BF)],
        [pltpu.VMEM((P_SIZE, KEEP_MAX), BF)],
        in_hbm(order), in_hbm(grad), in_hbm(query), in_hbm(key), in_hbm(value), in_hbm(weight), in_hbm(normed), vmem=24,
    )


def pick_kernel(info, counts, order, tokens, rows, pick):
    @pl.when(pl.program_id(0) == 0)
    def _():
        pick[...] = rows_by_token(order, counts[info[0]])

    rows[...] = dot(pick[...], tokens[0], (1, 0)).astype(BF)


def pick_rows(info, counts, order, tokens):
    width = tokens.shape[2]
    return call(
        pick_kernel, (width // 256,), (info, counts),
        [pl.BlockSpec((1, P_SIZE), lambda j, *_: (0, 0)), pl.BlockSpec((1, P_SIZE, 256), lambda j, *_: (0, 0, j))],
        pl.BlockSpec((KEEP_MAX, 256), lambda j, *_: (0, j)),
        jax.ShapeDtypeStruct((KEEP_MAX, width), BF),
        [pltpu.VMEM((KEEP_MAX, P_SIZE), BF)],
        order, tokens, vmem=12,
    )


def shift_of(y, core):
    return y if core == 0 else (8 - y if y else 4)


def cut_kernel(info, block, out):
    half = out.shape[2]
    out[0] = block[:, :half]
    out[1] = block[:, half:]


def fetch_columns(info, out_proj, chips):
    rows, full = out_proj.shape
    ranks = lax.axis_size("mp")
    width, part = full // ranks, rows // 4
    half = width // 2
    parts = call(
        cut_kernel, (1,), (info,),
        [pl.BlockSpec((part, width), lambda _, i: (i[3], lax.rem(i[1] + ranks - i[5], ranks)))],
        pl.BlockSpec((2, part, half), lambda _, i: (0, 0, 0)),
        jax.ShapeDtypeStruct((2, part, half), BF), [],
        in_hbm(out_proj), vmem=4,
    )
    table = [
        (dp_index(y, x, c) * ranks + m, dp_index(y, x, c) * ranks + (m - shift_of(y, c)) % ranks)
        for y, x, c in chips for m in range(ranks)
    ]
    got = lax.ppermute(parts, ("dp", "mp"), table)
    return got[0], got[1]


def spread_columns(parts, chips, after, beside):
    swap = [(dp_index(y, x, c), dp_index(y, x, 1 - c)) for y, x, c in chips]
    along = {
        "y": {s: [(dp_index(y, x, c), dp_index(y - s, x, c)) for y, x, c in chips] for s in STEPS[1:]},
        "x": {s: [(dp_index(y, x, c), dp_index(y, x - s, c)) for y, x, c in chips] for s in STEPS[1:]},
    }
    ways = (("y", "x"), ("x", "y"))
    first = [
        [part] + [lax.ppermute(part, "dp", along[way][s]) for s in STEPS[1:]]
        for part, (way, _) in zip(parts, ways)
    ]
    fours = [jnp.stack(pieces) for pieces in first]
    after, fours = lax.optimization_barrier((after, fours))
    done = beside(after)
    pieces = []
    for four, (_, way) in zip(fours, ways):
        for s in STEPS:
            piece = four if s == 0 else lax.ppermute(four, "dp", along[way][s])
            if way == "y" and s == STEPS[-1]:
                piece, *done = lax.optimization_barrier((piece, *done))
            pieces += [piece, lax.ppermute(piece, "dp", swap)]
    return pieces, done


def assemble_kernel(info, *refs):
    *pieces, out = refs
    ranks, rows, width = out.shape
    half, part = width // 2, rows // 4
    for stream in range(2):
        for at, second in enumerate(STEPS):
            for core in range(2):
                piece = pieces[(stream * 4 + at) * 2 + core]
                side = info[4] if core == 0 else 1 - info[4]
                for j, first in enumerate(STEPS):
                    dy, dx = (first, second) if stream == 0 else (second, first)
                    y, x = lax.rem(info[2] + 4 + dy, 4), lax.rem(info[3] + 4 + dx, 4)
                    shift = jnp.where(side == 0, y, jnp.where(y == 0, 4, 8 - y))
                    start = pl.multiple_of(x * part, 16)
                    out[lax.rem(info[1] + shift, ranks), pl.ds(start, part), stream * half:(stream + 1) * half] = piece[j]


def assemble(info, pieces, ranks):
    four, part, half = pieces[0].shape
    rows, width = four * part, 2 * half
    whole = call(
        assemble_kernel, (1,), (info,),
        [pl.BlockSpec((four, part, half), lambda _, i: (0, 0, 0))] * 16,
        pl.BlockSpec((ranks, rows, width), lambda _, i: (0, 0, 0)),
        pltpu.HBM((ranks, rows, width), BF), [],
        *pieces, vmem=24,
    )
    return whole.reshape(ranks * rows, width)


def project_kernel(info, mixed, weight, grad, gain, projected, sums):
    step = pl.program_id(0)
    part = dot(mixed[...], weight[...], (1, 0))

    @pl.when(step == 0)
    def _():
        projected[...] = part

    @pl.when(step > 0)
    def _():
        projected[...] += part

    @pl.when(step == pl.num_programs(0) - 1)
    def _():
        values = projected[...]
        scaled = grad[...].astype(F32) * gain[...].astype(F32)
        lane = lax.broadcasted_iota(jnp.int32, (KEEP_MAX, 128), 1)
        table = jnp.zeros((KEEP_MAX, 128), F32)
        for at, term in enumerate((values, values * values, scaled, scaled * values)):
            table = jnp.where(lane == at, jnp.sum(term, axis=-1, keepdims=True), table)
        sums[...] = jnp.transpose(table)[:8]


def project(info, mixed, weight, grad, gain):
    depth, width = weight.shape
    block = 768
    return call(
        project_kernel, (depth // block,), (info,),
        [
            pl.BlockSpec((KEEP_MAX, block), lambda k, i: (0, k)),
            pl.BlockSpec((block, width), lambda k, i: (k, 0)),
            pl.BlockSpec((KEEP_MAX, width), lambda k, i: (0, 0)),
            pl.BlockSpec((1, width), lambda k, i: (0, i[1])),
        ],
        [pl.BlockSpec((KEEP_MAX, width), lambda k, i: (0, 0)), pl.BlockSpec((8, KEEP_MAX), lambda k, i: (0, 0))],
        [jax.ShapeDtypeStruct((KEEP_MAX, width), F32), jax.ShapeDtypeStruct((8, KEEP_MAX), F32)],
        [], in_hbm(mixed), in_hbm(weight), grad, gain, vmem=18,
    )


def grad_kernel(full_width, info, counts, projected, grad, gain, *refs):
    *sums, grad_proj, normed = refs
    total = sums[0][...]
    for other in sums[1:]:
        total = total + other[...]
    total = jnp.concatenate([total, jnp.zeros((120, KEEP_MAX), F32)], axis=0)
    table = jnp.transpose(total) / full_width
    row_mean, row_square, first, cross = (table[:, at:at + 1] for at in range(4))
    inv_std = lax.rsqrt(row_square - row_mean * row_mean + 1e-06)
    second = (cross - row_mean * first) * inv_std
    live = lax.broadcasted_iota(jnp.int32, (KEEP_MAX, 1), 0) < counts[info[0]]
    gain_wide = gain[...].astype(F32)
    centred = (projected[...] - row_mean) * inv_std
    scaled = grad[...].astype(F32) * gain_wide
    normed[...] = jnp.where(live, centred * gain_wide, 0.0).astype(BF)
    grad_proj[...] = jnp.where(live, inv_std * (scaled - first - centred * second), 0.0).astype(BF)


def grad_rows(info, counts, projected, grad, gain, sums, full_width):
    width = projected.shape[1]
    whole = pl.BlockSpec((KEEP_MAX, width), lambda k, *i: (0, 0))
    shape = (KEEP_MAX, width)
    return call(
        functools.partial(grad_kernel, full_width), (1,), (info, counts),
        [whole, whole, pl.BlockSpec((1, width), lambda k, i, c: (0, i[1]))]
        + [pl.BlockSpec((8, KEEP_MAX), lambda k, *i: (0, 0))] * len(sums),
        [whole, whole], [pltpu.VMEM(shape, BF), pltpu.HBM(shape, BF)],
        [], projected, grad, gain, *sums, vmem=20,
    )


def back_kernel(grad_proj, weight, out):
    product = dot(grad_proj[...], weight[...], (1, 1)).astype(BF)
    half = out.shape[2]
    out[0] = product[:, :half]
    out[1] = product[:, half:]


def project_back(grad_proj, weight):
    depth, width = weight.shape
    block = 768
    return call(
        back_kernel, (depth // block,), (),
        [pl.BlockSpec((KEEP_MAX, width), lambda k: (0, 0)), pl.BlockSpec((block, width), lambda k: (k, 0))],
        pl.BlockSpec((2, KEEP_MAX, block // 2), lambda k: (k, 0, 0)),
        pltpu.HBM((depth * 2 // block, KEEP_MAX, block // 2), BF),
        [], grad_proj, in_vmem(weight), vmem=12,
    )


def outer_kernel(info, own_grad, other_grad, own_mixed, other_mixed, out, turned):
    @pl.when(pl.program_id(0) == 0)
    def _():
        turned[:, :KEEP_MAX] = jnp.transpose(own_grad[...])
        turned[:, KEEP_MAX:] = jnp.transpose(other_grad[...])

    rows = jnp.concatenate([own_mixed[...], other_mixed[...]], axis=0)
    out[0] = dot(turned[...], rows, (1, 0)).astype(BF)


def outer(info, own_grad, other_grad, mixed, other_mixed):
    width = own_grad.shape[1]
    block = mixed.shape[1] // 8
    grad_spec = pl.BlockSpec((KEEP_MAX, width), lambda j, i: (0, 0))
    return call(
        outer_kernel, (4,), (info,),
        [
            grad_spec, grad_spec,
            pl.BlockSpec((KEEP_MAX, block), lambda j, i: (0, i[4] * 4 + j)),
            pl.BlockSpec((KEEP_MAX, block), lambda j, i: (0, i[4] * 4 + j)),
        ],
        pl.BlockSpec((1, width, block), lambda j, i: (j, 0, 0)),
        jax.ShapeDtypeStruct((4, width, block), BF),
        [pltpu.VMEM((width, 2 * KEEP_MAX), BF)],
        own_grad, other_grad, in_hbm(mixed), in_hbm(other_mixed), vmem=16,
    )


def dp_index(y, x, core):
    return (y % 4) * 8 + (x % 4) * 2 + core


def on_device(
    query_heads, key_heads, value_heads, out_proj, norm_gain, keep_order, keep_count, cotangent
):
    ranks = lax.axis_size("mp")
    image = lax.axis_index("dp")
    rank = lax.axis_index("mp")
    y_at, core = image // 8, image % 2
    shift = jnp.where(core == 0, y_at, jnp.where(y_at == 0, 4, 8 - y_at))
    info = jnp.stack([image, rank, y_at, (image // 2) % 4, core, shift]).astype(jnp.int32)
    chips = [(y, x, core) for y in range(4) for x in range(4) for core in range(2)]
    swap = [(dp_index(y, x, c), dp_index(y, x, 1 - c)) for y, x, c in chips]

    parts = fetch_columns(info, out_proj, chips)
    mixed, query_c, key_c, value_c, weights = attend(
        info, keep_count, keep_order, query_heads, key_heads, value_heads
    )
    mixed, parts = lax.optimization_barrier((mixed, parts))
    mixed_all = lax.all_gather(mixed, "mp", axis=1, tiled=True)
    pieces, (grad_c, gain) = spread_columns(
        parts, chips, info,
        lambda after: (pick_rows(after, keep_count, keep_order, cotangent), norm_gain.reshape(1, -1)),
    )
    columns = assemble(info, pieces, ranks)
    mixed_all, grad_c, columns = lax.optimization_barrier((mixed_all, grad_c, columns))
    projected, sums = project(info, mixed_all, columns, grad_c, gain)
    def swapped(values, bits):
        return lax.ppermute(values, "mp", [(m, m ^ bits) for m in range(ranks)])

    four_sums = sums + swapped(sums, 1) + swapped(sums, 3) + swapped(sums, 2)
    all_sums = [four_sums, swapped(four_sums, 7)]
    other_mixed = lax.ppermute(mixed_all, "dp", swap)
    all_sums, other_mixed = lax.optimization_barrier((all_sums, other_mixed))
    grad_proj, normed_c = grad_rows(
        info, keep_count, projected, grad_c, gain, all_sums, norm_gain.shape[0]
    )
    mixed_grad = project_back(grad_proj, columns)
    other_grad = lax.ppermute(grad_proj, "dp", swap)
    mixed_grad, other_grad = lax.optimization_barrier((mixed_grad, other_grad))
    grad_mixed = lax.psum_scatter(mixed_grad, "mp", scatter_dimension=0, tiled=True)[0]

    pair = outer(info, grad_proj, other_grad, mixed_all, other_mixed)
    width, depth = pair.shape[1], pair.shape[2]
    pair = pair.reshape(16, width // 4, depth)
    groups = [[2 * j + c for j in range(16)] for c in range(2)]
    spread = lax.all_to_all(
        pair, "dp", split_axis=0, concat_axis=0, tiled=True, axis_index_groups=groups
    )
    total = jnp.sum(spread.astype(F32), axis=0).astype(BF)
    home = [
        (dp_index(y, x, c) * ranks + m, (4 * m + x) * ranks + 4 * c + y)
        for y, x, c in chips for m in range(ranks)
    ]
    total = lax.ppermute(total, ("dp", "mp"), home)

    *grads, normed = attend_back(
        info, keep_count, keep_order, grad_mixed, query_c, key_c, value_c, weights, normed_c
    )
    total, grads = lax.optimization_barrier((total, grads))
    return (normed, *grads, total.astype(F32).T)


def solution(mesh):
    in_specs = (
        P("dp", None, "mp"),
        P("dp", None, "mp"),
        P("dp", None, "mp"),
        P("mp", None),
        P(),
        P("dp", None),
        P(),
        P("dp", None, "mp"),
    )
    out_specs = (
        P("dp", None, "mp"),
        P("dp", None, "mp"),
        P("dp", None, "mp"),
        P("dp", None, "mp"),
        P("mp", "dp"),
    )
    return jax.shard_map(
        on_device, mesh=mesh, in_specs=in_specs, out_specs=out_specs, check_vma=False
    )
```

```python
import functools

import jax
import jax.numpy as jnp
from jax import lax
from jax.experimental import pallas as pl
from jax.experimental.pallas import tpu as pltpu
from jax.sharding import PartitionSpec as P

HEAD_DIM = 128
P_SIZE = 1024
KEEP_MAX = 512
MIB = 1024 * 1024
BF = jnp.bfloat16
F32 = jnp.float32
STEPS = (0, -1, 1, 2)


def call(kernel, grid, prefetched, in_specs, out_specs, out_shape, scratch, *operands, vmem):
    moved = 2 * sum(a.size * a.dtype.itemsize for a in operands)
    return pl.pallas_call(
        kernel,
        grid_spec=pltpu.PrefetchScalarGridSpec(
            num_scalar_prefetch=len(prefetched),
            grid=grid,
            in_specs=in_specs,
            out_specs=out_specs,
            scratch_shapes=scratch,
        ),
        out_shape=out_shape,
        compiler_params=pltpu.CompilerParams(vmem_limit_bytes=vmem * MIB),
        cost_estimate=pl.CostEstimate(flops=0, bytes_accessed=moved, transcendentals=0),
    )(*prefetched, *operands)


def in_hbm(x):
    return pltpu.with_memory_space_constraint(x, pltpu.HBM)


def in_vmem(x):
    return pltpu.with_memory_space_constraint(x, pltpu.VMEM)


def to_column(row):
    wide = jnp.broadcast_to(row, (128, row.shape[1]))
    return jnp.transpose(wide)[:, :1]


def rows_by_token(order_ref, live):
    token = to_column(order_ref[:, :KEEP_MAX].astype(F32)).astype(jnp.int32)
    row_at = lax.broadcasted_iota(jnp.int32, (KEEP_MAX, P_SIZE), 0)
    token_at = lax.broadcasted_iota(jnp.int32, (KEEP_MAX, P_SIZE), 1)
    return jnp.where((token == token_at) & (row_at < live), 1.0, 0.0).astype(BF)


def tokens_by_row(order_ref, live):
    token_at = lax.broadcasted_iota(jnp.int32, (P_SIZE, KEEP_MAX), 0)
    row_at = lax.broadcasted_iota(jnp.int32, (P_SIZE, KEEP_MAX), 1)
    hit = (order_ref[:, :KEEP_MAX] == token_at) & (row_at < live)
    return jnp.where(hit, 1.0, 0.0).astype(BF)


def dot(a, b, contract):
    return lax.dot_general(a, b, (((contract[0],), (contract[1],)), ((), ())), preferred_element_type=F32)


def attend_kernel(info, counts, order, query, key, value, mixed, query_c, key_c, value_c, weight, pick):
    live = counts[info[0]]

    @pl.when(pl.program_id(0) == 0)
    def _():
        pick[...] = rows_by_token(order, live)

    tokens = jnp.concatenate([query[0], key[0], value[0]], axis=1)
    rows = dot(pick[...], tokens, (1, 0)).astype(BF)
    q, k, v = rows[:, :128], rows[:, 128:256], rows[:, 256:]
    query_c[...], key_c[...], value_c[...] = q, k, v
    scores = dot(q, k, (1, 1)) * HEAD_DIM ** (-0.5)
    column = lax.broadcasted_iota(jnp.int32, (KEEP_MAX, KEEP_MAX), 1)
    scores = jnp.where(column < live, scores, -1000000000.0)
    exponent = jnp.exp(scores - jnp.max(scores, axis=-1, keepdims=True))
    w = exponent / jnp.sum(exponent, axis=-1, keepdims=True)
    weight[0] = w
    mixed[...] = dot(w.astype(BF), v, (1, 0)).astype(BF)


def attend(info, counts, order, query, key, value):
    heads = query.shape[2] // HEAD_DIM
    token_spec = pl.BlockSpec((1, P_SIZE, HEAD_DIM), lambda h, *_: (0, 0, h))
    row_spec = pl.BlockSpec((KEEP_MAX, HEAD_DIM), lambda h, *_: (0, h))
    row_shape = pltpu.HBM((KEEP_MAX, heads * HEAD_DIM), BF)
    return call(
        attend_kernel, (heads,), (info, counts),
        [pl.BlockSpec((1, P_SIZE), lambda h, *_: (0, 0)), token_spec, token_spec, token_spec],
        [row_spec] * 4 + [pl.BlockSpec((1, KEEP_MAX, KEEP_MAX), lambda h, *_: (h, 0, 0))],
        [row_shape] * 4 + [pltpu.HBM((heads, KEEP_MAX, KEEP_MAX), F32)],
        [pltpu.VMEM((KEEP_MAX, P_SIZE), BF)],
        in_hbm(order), in_hbm(query), in_hbm(key), in_hbm(value), vmem=20,
    )


def attend_back_kernel(
    info, counts, order, grad, query, key, value, weight, normed, grad_q, grad_k, grad_v, normed_out, place
):
    live = counts[info[0]]

    @pl.when(pl.program_id(0) == 0)
    def _():
        place[...] = tokens_by_row(order, live)

    g, q, k, v = grad[...], query[...], key[...], value[...]
    w = weight[0]
    d_weight = dot(g, v, (1, 1)).astype(BF).astype(F32)
    inner = jnp.sum(d_weight * w, axis=-1, keepdims=True)
    d_scores = (w * (d_weight - inner) * HEAD_DIM ** (-0.5)).astype(BF)
    dq = dot(d_scores, k, (1, 0)).astype(BF)
    dk = dot(d_scores, q, (0, 0)).astype(BF)
    dv = dot(w.astype(BF), g, (0, 0)).astype(BF)
    rows = jnp.concatenate([dq, dk, dv, normed[...]], axis=1)
    out = dot(place[...], rows, (1, 0)).astype(BF)
    grad_q[0], grad_k[0], grad_v[0] = out[:, :128], out[:, 128:256], out[:, 256:384]
    normed_out[0] = out[:, 384:]


def attend_back(info, counts, order, grad, query, key, value, weight, normed):
    heads = query.shape[1] // HEAD_DIM
    width = normed.shape[1]
    token_spec = pl.BlockSpec((1, P_SIZE, HEAD_DIM), lambda h, *_: (0, 0, h))
    row_spec = pl.BlockSpec((KEEP_MAX, HEAD_DIM), lambda h, *_: (0, h))
    token_shape = jax.ShapeDtypeStruct((1, P_SIZE, heads * HEAD_DIM), BF)
    return call(
        attend_back_kernel, (heads,), (info, counts),
        [pl.BlockSpec((1, P_SIZE), lambda h, *_: (0, 0))] + [row_spec] * 4
        + [pl.BlockSpec((1, KEEP_MAX, KEEP_MAX), lambda h, *_: (h, 0, 0)),
           pl.BlockSpec((KEEP_MAX, width // heads), lambda h, *_: (0, h))],
        [token_spec] * 3 + [pl.BlockSpec((1, P_SIZE, width // heads), lambda h, *_: (0, 0, h))],
        [token_shape] * 3 + [jax.ShapeDtypeStruct((1, P_SIZE, width), BF)],
        [pltpu.VMEM((P_SIZE, KEEP_MAX), BF)],
        in_hbm(order), in_hbm(grad), in_hbm(query), in_hbm(key), in_hbm(value), in_hbm(weight), in_hbm(normed), vmem=24,
    )


def pick_kernel(info, counts, order, tokens, rows, pick):
    @pl.when(pl.program_id(0) == 0)
    def _():
        pick[...] = rows_by_token(order, counts[info[0]])

    rows[...] = dot(pick[...], tokens[0], (1, 0)).astype(BF)


def pick_rows(info, counts, order, tokens):
    width = tokens.shape[2]
    return call(
        pick_kernel, (width // 256,), (info, counts),
        [pl.BlockSpec((1, P_SIZE), lambda j, *_: (0, 0)), pl.BlockSpec((1, P_SIZE, 256), lambda j, *_: (0, 0, j))],
        pl.BlockSpec((KEEP_MAX, 256), lambda j, *_: (0, j)),
        jax.ShapeDtypeStruct((KEEP_MAX, width), BF),
        [pltpu.VMEM((KEEP_MAX, P_SIZE), BF)],
        order, tokens, vmem=12,
    )


def shift_of(y, core):
    return y if core == 0 else (8 - y if y else 4)


def cut_kernel(info, block, out):
    half = out.shape[2]
    out[0] = block[:, :half]
    out[1] = block[:, half:]


def fetch_columns(info, out_proj, chips):
    rows, full = out_proj.shape
    ranks = lax.axis_size("mp")
    width, part = full // ranks, rows // 4
    half = width // 2
    parts = call(
        cut_kernel, (1,), (info,),
        [pl.BlockSpec((part, width), lambda _, i: (i[3], lax.rem(i[1] + ranks - i[5], ranks)))],
        pl.BlockSpec((2, part, half), lambda _, i: (0, 0, 0)),
        jax.ShapeDtypeStruct((2, part, half), BF), [],
        in_hbm(out_proj), vmem=4,
    )
    table = [
        (dp_index(y, x, c) * ranks + m, dp_index(y, x, c) * ranks + (m - shift_of(y, c)) % ranks)
        for y, x, c in chips for m in range(ranks)
    ]
    got = lax.ppermute(parts, ("dp", "mp"), table)
    return got[0], got[1]


def spread_columns(parts, chips, after, beside):
    swap = [(dp_index(y, x, c), dp_index(y, x, 1 - c)) for y, x, c in chips]
    along = {
        "y": {s: [(dp_index(y, x, c), dp_index(y - s, x, c)) for y, x, c in chips] for s in STEPS[1:]},
        "x": {s: [(dp_index(y, x, c), dp_index(y, x - s, c)) for y, x, c in chips] for s in STEPS[1:]},
    }
    ways = (("y", "x"), ("x", "y"))
    first = [
        [part] + [lax.ppermute(part, "dp", along[way][s]) for s in STEPS[1:]]
        for part, (way, _) in zip(parts, ways)
    ]
    fours = [jnp.stack(pieces) for pieces in first]
    after, fours = lax.optimization_barrier((after, fours))
    done = beside(after)
    pieces = []
    for four, (_, way) in zip(fours, ways):
        for s in STEPS:
            piece = four if s == 0 else lax.ppermute(four, "dp", along[way][s])
            if way == "y" and s == STEPS[-1]:
                piece, *done = lax.optimization_barrier((piece, *done))
            pieces += [piece, lax.ppermute(piece, "dp", swap)]
    return pieces, done


def assemble_kernel(info, *refs):
    *pieces, out = refs
    ranks, rows, width = out.shape
    half, part = width // 2, rows // 4
    for stream in range(2):
        for at, second in enumerate(STEPS):
            for core in range(2):
                piece = pieces[(stream * 4 + at) * 2 + core]
                side = info[4] if core == 0 else 1 - info[4]
                for j, first in enumerate(STEPS):
                    dy, dx = (first, second) if stream == 0 else (second, first)
                    y, x = lax.rem(info[2] + 4 + dy, 4), lax.rem(info[3] + 4 + dx, 4)
                    shift = jnp.where(side == 0, y, jnp.where(y == 0, 4, 8 - y))
                    start = pl.multiple_of(x * part, 16)
                    out[lax.rem(info[1] + shift, ranks), pl.ds(start, part), stream * half:(stream + 1) * half] = piece[j]


def assemble(info, pieces, ranks):
    four, part, half = pieces[0].shape
    rows, width = four * part, 2 * half
    whole = call(
        assemble_kernel, (1,), (info,),
        [pl.BlockSpec((four, part, half), lambda _, i: (0, 0, 0))] * 16,
        pl.BlockSpec((ranks, rows, width), lambda _, i: (0, 0, 0)),
        pltpu.HBM((ranks, rows, width), BF), [],
        *pieces, vmem=24,
    )
    return whole.reshape(ranks * rows, width)


def project_kernel(info, mixed, weight, grad, gain, projected, sums):
    step = pl.program_id(0)
    part = dot(mixed[...], weight[...], (1, 0))

    @pl.when(step == 0)
    def _():
        projected[...] = part

    @pl.when(step > 0)
    def _():
        projected[...] += part

    @pl.when(step == pl.num_programs(0) - 1)
    def _():
        values = projected[...]
        scaled = grad[...].astype(F32) * gain[...].astype(F32)
        lane = lax.broadcasted_iota(jnp.int32, (KEEP_MAX, 128), 1)
        table = jnp.zeros((KEEP_MAX, 128), F32)
        for at, term in enumerate((values, values * values, scaled, scaled * values)):
            table = jnp.where(lane == at, jnp.sum(term, axis=-1, keepdims=True), table)
        sums[...] = jnp.transpose(table)[:8]


def project(info, mixed, weight, grad, gain):
    depth, width = weight.shape
    block = 1536
    return call(
        project_kernel, (depth // block,), (info,),
        [
            pl.BlockSpec((KEEP_MAX, block), lambda k, i: (0, k)),
            pl.BlockSpec((block, width), lambda k, i: (k, 0)),
            pl.BlockSpec((KEEP_MAX, width), lambda k, i: (0, 0)),
            pl.BlockSpec((1, width), lambda k, i: (0, i[1])),
        ],
        [pl.BlockSpec((KEEP_MAX, width), lambda k, i: (0, 0)), pl.BlockSpec((8, KEEP_MAX), lambda k, i: (0, 0))],
        [jax.ShapeDtypeStruct((KEEP_MAX, width), F32), jax.ShapeDtypeStruct((8, KEEP_MAX), F32)],
        [], in_hbm(mixed), in_hbm(weight), grad, gain, vmem=26,
    )


def grad_kernel(full_width, info, counts, projected, grad, gain, *refs):
    *sums, grad_proj, normed = refs
    total = sums[0][...]
    for other in sums[1:]:
        total = total + other[...]
    total = jnp.concatenate([total, jnp.zeros((120, KEEP_MAX), F32)], axis=0)
    table = jnp.transpose(total) / full_width
    row_mean, row_square, first, cross = (table[:, at:at + 1] for at in range(4))
    inv_std = lax.rsqrt(row_square - row_mean * row_mean + 1e-06)
    second = (cross - row_mean * first) * inv_std
    live = lax.broadcasted_iota(jnp.int32, (KEEP_MAX, 1), 0) < counts[info[0]]
    gain_wide = gain[...].astype(F32)
    centred = (projected[...] - row_mean) * inv_std
    scaled = grad[...].astype(F32) * gain_wide
    normed[...] = jnp.where(live, centred * gain_wide, 0.0).astype(BF)
    grad_proj[...] = jnp.where(live, inv_std * (scaled - first - centred * second), 0.0).astype(BF)


def grad_rows(info, counts, projected, grad, gain, sums, full_width):
    width = projected.shape[1]
    whole = pl.BlockSpec((KEEP_MAX, width), lambda k, *i: (0, 0))
    shape = (KEEP_MAX, width)
    return call(
        functools.partial(grad_kernel, full_width), (1,), (info, counts),
        [whole, whole, pl.BlockSpec((1, width), lambda k, i, c: (0, i[1]))]
        + [pl.BlockSpec((8, KEEP_MAX), lambda k, *i: (0, 0))] * len(sums),
        [whole, whole], [pltpu.VMEM(shape, BF), pltpu.HBM(shape, BF)],
        [], projected, grad, gain, *sums, vmem=20,
    )


def back_kernel(grad_proj, weight, out):
    product = dot(grad_proj[...], weight[...], (1, 1)).astype(BF)
    half = out.shape[2]
    out[0] = product[:, :half]
    out[1] = product[:, half:]


def project_back(grad_proj, weight):
    depth, width = weight.shape
    block = 768
    return call(
        back_kernel, (depth // block,), (),
        [pl.BlockSpec((KEEP_MAX, width), lambda k: (0, 0)), pl.BlockSpec((block, width), lambda k: (k, 0))],
        pl.BlockSpec((2, KEEP_MAX, block // 2), lambda k: (k, 0, 0)),
        pltpu.HBM((depth * 2 // block, KEEP_MAX, block // 2), BF),
        [], grad_proj, in_vmem(weight), vmem=12,
    )


def outer_kernel(info, own_grad, other_grad, own_mixed, other_mixed, out, turned):
    @pl.when(pl.program_id(0) == 0)
    def _():
        turned[:, :KEEP_MAX] = jnp.transpose(own_grad[...])
        turned[:, KEEP_MAX:] = jnp.transpose(other_grad[...])

    product = dot(turned[:, :KEEP_MAX], own_mixed[...], (1, 0))
    product = product + dot(turned[:, KEEP_MAX:], other_mixed[...], (1, 0))
    width = out.shape[2]
    for j in range(out.shape[0]):
        out[j] = product[:, j * width:(j + 1) * width].astype(BF)


def outer(info, own_grad, other_grad, mixed, other_mixed):
    width = own_grad.shape[1]
    block = mixed.shape[1] // 8
    grad_spec = pl.BlockSpec((KEEP_MAX, width), lambda j, i: (0, 0))
    mixed_spec = pl.BlockSpec((KEEP_MAX, 2 * block), lambda j, i: (0, i[4] * 2 + j))
    return call(
        outer_kernel, (2,), (info,),
        [grad_spec, grad_spec, mixed_spec, mixed_spec],
        pl.BlockSpec((2, width, block), lambda j, i: (j, 0, 0)),
        jax.ShapeDtypeStruct((4, width, block), BF),
        [pltpu.VMEM((width, 2 * KEEP_MAX), BF)],
        own_grad, other_grad, in_hbm(mixed), in_hbm(other_mixed), vmem=22,
    )


def dp_index(y, x, core):
    return (y % 4) * 8 + (x % 4) * 2 + core


def on_device(
    query_heads, key_heads, value_heads, out_proj, norm_gain, keep_order, keep_count, cotangent
):
    ranks = lax.axis_size("mp")
    image = lax.axis_index("dp")
    rank = lax.axis_index("mp")
    y_at, core = image // 8, image % 2
    shift = jnp.where(core == 0, y_at, jnp.where(y_at == 0, 4, 8 - y_at))
    info = jnp.stack([image, rank, y_at, (image // 2) % 4, core, shift]).astype(jnp.int32)
    chips = [(y, x, core) for y in range(4) for x in range(4) for core in range(2)]
    swap = [(dp_index(y, x, c), dp_index(y, x, 1 - c)) for y, x, c in chips]

    parts = fetch_columns(info, out_proj, chips)
    mixed, query_c, key_c, value_c, weights = attend(
        info, keep_count, keep_order, query_heads, key_heads, value_heads
    )
    mixed, parts = lax.optimization_barrier((mixed, parts))
    mixed_all = lax.all_gather(mixed, "mp", axis=1, tiled=True)
    pieces, (grad_c, gain) = spread_columns(
        parts, chips, info,
        lambda after: (pick_rows(after, keep_count, keep_order, cotangent), norm_gain.reshape(1, -1)),
    )
    columns = assemble(info, pieces, ranks)
    mixed_all, grad_c, columns = lax.optimization_barrier((mixed_all, grad_c, columns))
    projected, sums = project(info, mixed_all, columns, grad_c, gain)
    def swapped(values, bits):
        return lax.ppermute(values, "mp", [(m, m ^ bits) for m in range(ranks)])

    four_sums = sums + swapped(sums, 1) + swapped(sums, 3) + swapped(sums, 2)
    all_sums = [four_sums, swapped(four_sums, 7)]
    other_mixed = lax.ppermute(mixed_all, "dp", swap)
    all_sums, other_mixed = lax.optimization_barrier((all_sums, other_mixed))
    grad_proj, normed_c = grad_rows(
        info, keep_count, projected, grad_c, gain, all_sums, norm_gain.shape[0]
    )
    mixed_grad = project_back(grad_proj, columns)
    other_grad = lax.ppermute(grad_proj, "dp", swap)
    mixed_grad, other_grad = lax.optimization_barrier((mixed_grad, other_grad))
    grad_mixed = lax.psum_scatter(mixed_grad, "mp", scatter_dimension=0, tiled=True)[0]

    pair = outer(info, grad_proj, other_grad, mixed_all, other_mixed)
    width, depth = pair.shape[1], pair.shape[2]
    pair = pair.reshape(16, width // 4, depth)
    groups = [[2 * j + c for j in range(16)] for c in range(2)]
    spread = lax.all_to_all(
        pair, "dp", split_axis=0, concat_axis=0, tiled=True, axis_index_groups=groups
    )
    total = jnp.sum(spread.astype(F32), axis=0).astype(BF)
    home = [
        (dp_index(y, x, c) * ranks + m, (4 * m + x) * ranks + 4 * c + y)
        for y, x, c in chips for m in range(ranks)
    ]
    total = lax.ppermute(total, ("dp", "mp"), home)

    *grads, normed = attend_back(
        info, keep_count, keep_order, grad_mixed, query_c, key_c, value_c, weights, normed_c
    )
    total, grads = lax.optimization_barrier((total, grads))
    return (normed, *grads, total.astype(F32).T)


def solution(mesh):
    in_specs = (
        P("dp", None, "mp"),
        P("dp", None, "mp"),
        P("dp", None, "mp"),
        P("mp", None),
        P(),
        P("dp", None),
        P(),
        P("dp", None, "mp"),
    )
    out_specs = (
        P("dp", None, "mp"),
        P("dp", None, "mp"),
        P("dp", None, "mp"),
        P("dp", None, "mp"),
        P("mp", "dp"),
    )
    return jax.shard_map(
        on_device, mesh=mesh, in_specs=in_specs, out_specs=out_specs, check_vma=False
    )
```

```python
import functools

import jax
import jax.numpy as jnp
from jax import lax
from jax.experimental import pallas as pl
from jax.experimental.pallas import tpu as pltpu
from jax.sharding import PartitionSpec as P

HEAD_DIM = 128
P_SIZE = 1024
KEEP_MAX = 512
MIB = 1024 * 1024
BF = jnp.bfloat16
F32 = jnp.float32
STEPS = (0, -1, 1, 2)


def call(kernel, grid, prefetched, in_specs, out_specs, out_shape, scratch, *operands, vmem):
    moved = 2 * sum(a.size * a.dtype.itemsize for a in operands)
    return pl.pallas_call(
        kernel,
        grid_spec=pltpu.PrefetchScalarGridSpec(
            num_scalar_prefetch=len(prefetched),
            grid=grid,
            in_specs=in_specs,
            out_specs=out_specs,
            scratch_shapes=scratch,
        ),
        out_shape=out_shape,
        compiler_params=pltpu.CompilerParams(vmem_limit_bytes=vmem * MIB),
        cost_estimate=pl.CostEstimate(flops=0, bytes_accessed=moved, transcendentals=0),
    )(*prefetched, *operands)


def in_hbm(x):
    return pltpu.with_memory_space_constraint(x, pltpu.HBM)


def in_vmem(x):
    return pltpu.with_memory_space_constraint(x, pltpu.VMEM)


def to_column(row):
    wide = jnp.broadcast_to(row, (128, row.shape[1]))
    return jnp.transpose(wide)[:, :1]


def rows_by_token(order_ref, live):
    token = to_column(order_ref[:, :KEEP_MAX].astype(F32)).astype(jnp.int32)
    token = jnp.where(lax.broadcasted_iota(jnp.int32, (KEEP_MAX, 1), 0) < live, token, -1)
    token_at = lax.broadcasted_iota(jnp.int32, (KEEP_MAX, P_SIZE), 1)
    return jnp.where(token == token_at, 1.0, 0.0).astype(BF)


def tokens_by_row(order_ref, live):
    token_at = lax.broadcasted_iota(jnp.int32, (P_SIZE, KEEP_MAX), 0)
    row_at = lax.broadcasted_iota(jnp.int32, (1, KEEP_MAX), 1)
    token = jnp.where(row_at < live, order_ref[:, :KEEP_MAX], -1)
    return jnp.where(token == token_at, 1.0, 0.0).astype(BF)


def dot(a, b, contract):
    return lax.dot_general(a, b, (((contract[0],), (contract[1],)), ((), ())), preferred_element_type=F32)


def attend_kernel(info, counts, order, query, key, value, mixed, query_c, key_c, value_c, weight, pick):
    live = counts[info[0]]

    @pl.when(pl.program_id(0) == 0)
    def _():
        pick[...] = rows_by_token(order, live)

    tokens = jnp.concatenate([query[0], key[0], value[0]], axis=1)
    rows = dot(pick[...], tokens, (1, 0)).astype(BF)
    q, k, v = rows[:, :128], rows[:, 128:256], rows[:, 256:]
    query_c[...], key_c[...], value_c[...] = q, k, v
    scores = dot(q, k, (1, 1)) * HEAD_DIM ** (-0.5)
    column = lax.broadcasted_iota(jnp.int32, (KEEP_MAX, KEEP_MAX), 1)
    scores = jnp.where(column < live, scores, -1000000000.0)
    exponent = jnp.exp(scores - jnp.max(scores, axis=-1, keepdims=True))
    w = exponent * (1.0 / jnp.sum(exponent, axis=-1, keepdims=True))
    weight[0] = w
    mixed[...] = dot(w.astype(BF), v, (1, 0)).astype(BF)


def attend(info, counts, order, query, key, value):
    heads = query.shape[2] // HEAD_DIM
    token_spec = pl.BlockSpec((1, P_SIZE, HEAD_DIM), lambda h, *_: (0, 0, h))
    row_spec = pl.BlockSpec((KEEP_MAX, HEAD_DIM), lambda h, *_: (0, h))
    row_shape = pltpu.HBM((KEEP_MAX, heads * HEAD_DIM), BF)
    return call(
        attend_kernel, (heads,), (info, counts),
        [pl.BlockSpec((1, P_SIZE), lambda h, *_: (0, 0)), token_spec, token_spec, token_spec],
        [row_spec] * 4 + [pl.BlockSpec((1, KEEP_MAX, KEEP_MAX), lambda h, *_: (h, 0, 0))],
        [row_shape] * 4 + [pltpu.HBM((heads, KEEP_MAX, KEEP_MAX), F32)],
        [pltpu.VMEM((KEEP_MAX, P_SIZE), BF)],
        in_hbm(order), in_hbm(query), in_hbm(key), in_hbm(value), vmem=20,
    )


def attend_back_kernel(
    info, counts, order, grad, query, key, value, weight, normed, grad_q, grad_k, grad_v, normed_out, place
):
    live = counts[info[0]]

    @pl.when(pl.program_id(0) == 0)
    def _():
        place[...] = tokens_by_row(order, live)

    g, q, k, v = grad[...], query[...], key[...], value[...]
    w = weight[0]
    d_weight = dot(g, v, (1, 1)).astype(BF).astype(F32)
    inner = jnp.sum(d_weight * w, axis=-1, keepdims=True)
    d_scores = (w * (d_weight - inner) * HEAD_DIM ** (-0.5)).astype(BF)
    dq = dot(d_scores, k, (1, 0)).astype(BF)
    dk = dot(d_scores, q, (0, 0)).astype(BF)
    dv = dot(w.astype(BF), g, (0, 0)).astype(BF)
    rows = jnp.concatenate([dq, dk, dv, normed[...]], axis=1)
    out = dot(place[...], rows, (1, 0)).astype(BF)
    grad_q[0], grad_k[0], grad_v[0] = out[:, :128], out[:, 128:256], out[:, 256:384]
    normed_out[0] = out[:, 384:]


def attend_back(info, counts, order, grad, query, key, value, weight, normed):
    heads = query.shape[1] // HEAD_DIM
    width = normed.shape[1]
    token_spec = pl.BlockSpec((1, P_SIZE, HEAD_DIM), lambda h, *_: (0, 0, h))
    row_spec = pl.BlockSpec((KEEP_MAX, HEAD_DIM), lambda h, *_: (0, h))
    token_shape = jax.ShapeDtypeStruct((1, P_SIZE, heads * HEAD_DIM), BF)
    return call(
        attend_back_kernel, (heads,), (info, counts),
        [pl.BlockSpec((1, P_SIZE), lambda h, *_: (0, 0))] + [row_spec] * 4
        + [pl.BlockSpec((1, KEEP_MAX, KEEP_MAX), lambda h, *_: (h, 0, 0)),
           pl.BlockSpec((KEEP_MAX, width // heads), lambda h, *_: (0, h))],
        [token_spec] * 3 + [pl.BlockSpec((1, P_SIZE, width // heads), lambda h, *_: (0, 0, h))],
        [token_shape] * 3 + [jax.ShapeDtypeStruct((1, P_SIZE, width), BF)],
        [pltpu.VMEM((P_SIZE, KEEP_MAX), BF)],
        in_hbm(order), in_hbm(grad), in_hbm(query), in_hbm(key), in_hbm(value), in_hbm(weight), in_hbm(normed), vmem=24,
    )


def pick_kernel(info, counts, order, tokens, rows, pick):
    @pl.when(pl.program_id(0) == 0)
    def _():
        pick[...] = rows_by_token(order, counts[info[0]])

    rows[...] = dot(pick[...], tokens[0], (1, 0)).astype(BF)


def pick_rows(info, counts, order, tokens):
    width = tokens.shape[2]
    return call(
        pick_kernel, (width // 256,), (info, counts),
        [pl.BlockSpec((1, P_SIZE), lambda j, *_: (0, 0)), pl.BlockSpec((1, P_SIZE, 256), lambda j, *_: (0, 0, j))],
        pl.BlockSpec((KEEP_MAX, 256), lambda j, *_: (0, j)),
        jax.ShapeDtypeStruct((KEEP_MAX, width), BF),
        [pltpu.VMEM((KEEP_MAX, P_SIZE), BF)],
        order, tokens, vmem=12,
    )


def shift_of(y, core):
    return y if core == 0 else (8 - y if y else 4)


def cut_kernel(info, block, out):
    half = out.shape[2]
    out[0] = block[:, :half]
    out[1] = block[:, half:]


def fetch_columns(info, out_proj, chips):
    rows, full = out_proj.shape
    ranks = lax.axis_size("mp")
    width, part = full // ranks, rows // 4
    half = width // 2
    parts = call(
        cut_kernel, (1,), (info,),
        [pl.BlockSpec((part, width), lambda _, i: (i[3], lax.rem(i[1] + ranks - i[5], ranks)))],
        pl.BlockSpec((2, part, half), lambda _, i: (0, 0, 0)),
        jax.ShapeDtypeStruct((2, part, half), BF), [],
        in_hbm(out_proj), vmem=4,
    )
    table = [
        (dp_index(y, x, c) * ranks + m, dp_index(y, x, c) * ranks + (m - shift_of(y, c)) % ranks)
        for y, x, c in chips for m in range(ranks)
    ]
    got = lax.ppermute(parts, ("dp", "mp"), table)
    return got[0], got[1]


def spread_columns(parts, chips, after, beside):
    swap = [(dp_index(y, x, c), dp_index(y, x, 1 - c)) for y, x, c in chips]
    along = {
        "y": {s: [(dp_index(y, x, c), dp_index(y - s, x, c)) for y, x, c in chips] for s in STEPS[1:]},
        "x": {s: [(dp_index(y, x, c), dp_index(y, x - s, c)) for y, x, c in chips] for s in STEPS[1:]},
    }
    ways = (("y", "x"), ("x", "y"))
    first = [
        [part] + [lax.ppermute(part, "dp", along[way][s]) for s in STEPS[1:]]
        for part, (way, _) in zip(parts, ways)
    ]
    fours = [jnp.stack(pieces) for pieces in first]
    after, fours = lax.optimization_barrier((after, fours))
    done = beside(after)
    pieces = []
    for four, (_, way) in zip(fours, ways):
        for s in STEPS:
            piece = four if s == 0 else lax.ppermute(four, "dp", along[way][s])
            if way == "y" and s == STEPS[-1]:
                piece, *done = lax.optimization_barrier((piece, *done))
            pieces += [piece, lax.ppermute(piece, "dp", swap)]
    return pieces, done


def assemble_kernel(info, *refs):
    *pieces, out = refs
    ranks, rows, width = out.shape
    half, part = width // 2, rows // 4
    for stream in range(2):
        for at, second in enumerate(STEPS):
            for core in range(2):
                piece = pieces[(stream * 4 + at) * 2 + core]
                side = info[4] if core == 0 else 1 - info[4]
                for j, first in enumerate(STEPS):
                    dy, dx = (first, second) if stream == 0 else (second, first)
                    y, x = lax.rem(info[2] + 4 + dy, 4), lax.rem(info[3] + 4 + dx, 4)
                    shift = jnp.where(side == 0, y, jnp.where(y == 0, 4, 8 - y))
                    start = pl.multiple_of(x * part, 16)
                    out[lax.rem(info[1] + shift, ranks), pl.ds(start, part), stream * half:(stream + 1) * half] = piece[j]


def assemble(info, pieces, ranks):
    four, part, half = pieces[0].shape
    rows, width = four * part, 2 * half
    whole = call(
        assemble_kernel, (1,), (info,),
        [pl.BlockSpec((four, part, half), lambda _, i: (0, 0, 0))] * 16,
        pl.BlockSpec((ranks, rows, width), lambda _, i: (0, 0, 0)),
        pltpu.HBM((ranks, rows, width), BF), [],
        *pieces, vmem=24,
    )
    return whole.reshape(ranks * rows, width)


def project_kernel(info, mixed, weight, grad, gain, projected, sums):
    step = pl.program_id(0)
    part = dot(mixed[...], weight[...], (1, 0))

    @pl.when(step == 0)
    def _():
        projected[...] = part

    @pl.when(step > 0)
    def _():
        projected[...] += part

    @pl.when(step == pl.num_programs(0) - 1)
    def _():
        values = projected[...]
        scaled = grad[...].astype(F32) * gain[...].astype(F32)
        lane = lax.broadcasted_iota(jnp.int32, (KEEP_MAX, 128), 1)
        table = jnp.zeros((KEEP_MAX, 128), F32)
        for at, term in enumerate((values, values * values, scaled, scaled * values)):
            table = jnp.where(lane == at, jnp.sum(term, axis=-1, keepdims=True), table)
        sums[...] = jnp.transpose(table)[:8]


def project(info, mixed, weight, grad, gain):
    depth, width = weight.shape
    block = 1536
    return call(
        project_kernel, (depth // block,), (info,),
        [
            pl.BlockSpec((KEEP_MAX, block), lambda k, i: (0, k)),
            pl.BlockSpec((block, width), lambda k, i: (k, 0)),
            pl.BlockSpec((KEEP_MAX, width), lambda k, i: (0, 0)),
            pl.BlockSpec((1, width), lambda k, i: (0, i[1])),
        ],
        [pl.BlockSpec((KEEP_MAX, width), lambda k, i: (0, 0)), pl.BlockSpec((8, KEEP_MAX), lambda k, i: (0, 0))],
        [jax.ShapeDtypeStruct((KEEP_MAX, width), F32), jax.ShapeDtypeStruct((8, KEEP_MAX), F32)],
        [], in_hbm(mixed), in_hbm(weight), grad, gain, vmem=26,
    )


def grad_kernel(full_width, info, counts, projected, grad, gain, *refs):
    *sums, grad_proj, normed = refs
    total = sums[0][...]
    for other in sums[1:]:
        total = total + other[...]
    total = jnp.concatenate([total, jnp.zeros((120, KEEP_MAX), F32)], axis=0)
    table = jnp.transpose(total) / full_width
    row_mean, row_square, first, cross = (table[:, at:at + 1] for at in range(4))
    inv_std = lax.rsqrt(row_square - row_mean * row_mean + 1e-06)
    second = (cross - row_mean * first) * inv_std
    live = lax.broadcasted_iota(jnp.int32, (KEEP_MAX, 1), 0) < counts[info[0]]
    gain_wide = gain[...].astype(F32)
    centred = (projected[...] - row_mean) * inv_std
    scaled = grad[...].astype(F32) * gain_wide
    normed[...] = jnp.where(live, centred * gain_wide, 0.0).astype(BF)
    grad_proj[...] = jnp.where(live, inv_std * (scaled - first - centred * second), 0.0).astype(BF)


def grad_rows(info, counts, projected, grad, gain, sums, full_width):
    width = projected.shape[1]
    whole = pl.BlockSpec((KEEP_MAX, width), lambda k, *i: (0, 0))
    shape = (KEEP_MAX, width)
    return call(
        functools.partial(grad_kernel, full_width), (1,), (info, counts),
        [whole, whole, pl.BlockSpec((1, width), lambda k, i, c: (0, i[1]))]
        + [pl.BlockSpec((8, KEEP_MAX), lambda k, *i: (0, 0))] * len(sums),
        [whole, whole], [pltpu.VMEM(shape, BF), pltpu.HBM(shape, BF)],
        [], projected, grad, gain, *sums, vmem=20,
    )


def back_kernel(grad_proj, weight, out):
    product = dot(grad_proj[...], weight[...], (1, 1)).astype(BF)
    half = out.shape[2]
    out[0] = product[:, :half]
    out[1] = product[:, half:]


def project_back(grad_proj, weight):
    depth, width = weight.shape
    block = 768
    return call(
        back_kernel, (depth // block,), (),
        [pl.BlockSpec((KEEP_MAX, width), lambda k: (0, 0)), pl.BlockSpec((block, width), lambda k: (k, 0))],
        pl.BlockSpec((2, KEEP_MAX, block // 2), lambda k: (k, 0, 0)),
        pltpu.HBM((depth * 2 // block, KEEP_MAX, block // 2), BF),
        [], grad_proj, in_vmem(weight), vmem=12,
    )


def outer_kernel(info, own_grad, other_grad, own_mixed, other_mixed, out, turned):
    @pl.when(pl.program_id(0) == 0)
    def _():
        turned[:, :KEEP_MAX] = jnp.transpose(own_grad[...])
        turned[:, KEEP_MAX:] = jnp.transpose(other_grad[...])

    product = dot(turned[:, :KEEP_MAX], own_mixed[...], (1, 0))
    product = product + dot(turned[:, KEEP_MAX:], other_mixed[...], (1, 0))
    width = out.shape[2]
    for j in range(out.shape[0]):
        out[j] = product[:, j * width:(j + 1) * width].astype(BF)


def outer(info, own_grad, other_grad, mixed, other_mixed):
    width = own_grad.shape[1]
    block = mixed.shape[1] // 8
    grad_spec = pl.BlockSpec((KEEP_MAX, width), lambda j, i: (0, 0))
    mixed_spec = pl.BlockSpec((KEEP_MAX, 2 * block), lambda j, i: (0, i[4] * 2 + j))
    return call(
        outer_kernel, (2,), (info,),
        [grad_spec, grad_spec, mixed_spec, mixed_spec],
        pl.BlockSpec((2, width, block), lambda j, i: (j, 0, 0)),
        jax.ShapeDtypeStruct((4, width, block), BF),
        [pltpu.VMEM((width, 2 * KEEP_MAX), BF)],
        own_grad, other_grad, in_hbm(mixed), in_hbm(other_mixed), vmem=22,
    )


def dp_index(y, x, core):
    return (y % 4) * 8 + (x % 4) * 2 + core


def on_device(
    query_heads, key_heads, value_heads, out_proj, norm_gain, keep_order, keep_count, cotangent
):
    ranks = lax.axis_size("mp")
    image = lax.axis_index("dp")
    rank = lax.axis_index("mp")
    y_at, core = image // 8, image % 2
    shift = jnp.where(core == 0, y_at, jnp.where(y_at == 0, 4, 8 - y_at))
    info = jnp.stack([image, rank, y_at, (image // 2) % 4, core, shift]).astype(jnp.int32)
    chips = [(y, x, core) for y in range(4) for x in range(4) for core in range(2)]
    swap = [(dp_index(y, x, c), dp_index(y, x, 1 - c)) for y, x, c in chips]

    parts = fetch_columns(info, out_proj, chips)
    mixed, query_c, key_c, value_c, weights = attend(
        info, keep_count, keep_order, query_heads, key_heads, value_heads
    )
    mixed, parts = lax.optimization_barrier((mixed, parts))
    mixed_all = lax.all_gather(mixed, "mp", axis=1, tiled=True)
    pieces, (grad_c, gain) = spread_columns(
        parts, chips, info,
        lambda after: (pick_rows(after, keep_count, keep_order, cotangent), norm_gain.reshape(1, -1)),
    )
    columns = assemble(info, pieces, ranks)
    mixed_all, grad_c, columns = lax.optimization_barrier((mixed_all, grad_c, columns))
    projected, sums = project(info, mixed_all, columns, grad_c, gain)
    columns, sums = lax.optimization_barrier((columns, sums))

    def swapped(values, bits):
        return lax.ppermute(values, "mp", [(m, m ^ bits) for m in range(ranks)])

    four_sums = sums + swapped(sums, 1) + swapped(sums, 3) + swapped(sums, 2)
    all_sums = [four_sums, swapped(four_sums, 7)]
    other_mixed = lax.ppermute(mixed_all, "dp", swap)
    all_sums, other_mixed = lax.optimization_barrier((all_sums, other_mixed))
    grad_proj, normed_c = grad_rows(
        info, keep_count, projected, grad_c, gain, all_sums, norm_gain.shape[0]
    )
    mixed_grad = project_back(grad_proj, columns)
    other_grad = lax.ppermute(grad_proj, "dp", swap)
    mixed_grad, other_grad = lax.optimization_barrier((mixed_grad, other_grad))
    grad_mixed = lax.psum_scatter(mixed_grad, "mp", scatter_dimension=0, tiled=True)[0]

    pair = outer(info, grad_proj, other_grad, mixed_all, other_mixed)
    width, depth = pair.shape[1], pair.shape[2]
    pair = pair.reshape(16, width // 4, depth)
    groups = [[2 * j + c for j in range(16)] for c in range(2)]
    spread = lax.all_to_all(
        pair, "dp", split_axis=0, concat_axis=0, tiled=True, axis_index_groups=groups
    )
    total = jnp.sum(spread.astype(F32), axis=0).astype(BF)
    home = [
        (dp_index(y, x, c) * ranks + m, (4 * m + x) * ranks + 4 * c + y)
        for y, x, c in chips for m in range(ranks)
    ]
    total = lax.ppermute(total, ("dp", "mp"), home)

    *grads, normed = attend_back(
        info, keep_count, keep_order, grad_mixed, query_c, key_c, value_c, weights, normed_c
    )
    total, grads = lax.optimization_barrier((total, grads))
    return (normed, *grads, total.astype(F32).T)


def solution(mesh):
    in_specs = (
        P("dp", None, "mp"),
        P("dp", None, "mp"),
        P("dp", None, "mp"),
        P("mp", None),
        P(),
        P("dp", None),
        P(),
        P("dp", None, "mp"),
    )
    out_specs = (
        P("dp", None, "mp"),
        P("dp", None, "mp"),
        P("dp", None, "mp"),
        P("dp", None, "mp"),
        P("mp", "dp"),
    )
    return jax.shard_map(
        on_device, mesh=mesh, in_specs=in_specs, out_specs=out_specs, check_vma=False
    )
```

```python
import functools

import jax
import jax.numpy as jnp
from jax import lax
from jax.experimental import pallas as pl
from jax.experimental.pallas import tpu as pltpu
from jax.sharding import PartitionSpec as P

HEAD_DIM = 128
P_SIZE = 1024
KEEP_MAX = 512
MIB = 1024 * 1024
BF = jnp.bfloat16
F32 = jnp.float32
STEPS = (0, -1, 1, 2)


def call(kernel, grid, prefetched, in_specs, out_specs, out_shape, scratch, *operands, vmem):
    moved = 2 * sum(a.size * a.dtype.itemsize for a in operands)
    return pl.pallas_call(
        kernel,
        grid_spec=pltpu.PrefetchScalarGridSpec(
            num_scalar_prefetch=len(prefetched),
            grid=grid,
            in_specs=in_specs,
            out_specs=out_specs,
            scratch_shapes=scratch,
        ),
        out_shape=out_shape,
        compiler_params=pltpu.CompilerParams(vmem_limit_bytes=vmem * MIB),
        cost_estimate=pl.CostEstimate(flops=0, bytes_accessed=moved, transcendentals=0),
    )(*prefetched, *operands)


def in_hbm(x):
    return pltpu.with_memory_space_constraint(x, pltpu.HBM)


def in_vmem(x):
    return pltpu.with_memory_space_constraint(x, pltpu.VMEM)


def to_column(row):
    wide = jnp.broadcast_to(row, (128, row.shape[1]))
    return jnp.transpose(wide)[:, :1]


def rows_by_token(order_ref, live):
    token = to_column(order_ref[:, :KEEP_MAX].astype(F32)).astype(jnp.int32)
    row_at = lax.broadcasted_iota(jnp.int32, (KEEP_MAX, P_SIZE), 0)
    token_at = lax.broadcasted_iota(jnp.int32, (KEEP_MAX, P_SIZE), 1)
    return jnp.where((token == token_at) & (row_at < live), 1.0, 0.0).astype(BF)


def tokens_by_row(order_ref, live):
    token_at = lax.broadcasted_iota(jnp.int32, (P_SIZE, KEEP_MAX), 0)
    row_at = lax.broadcasted_iota(jnp.int32, (P_SIZE, KEEP_MAX), 1)
    hit = (order_ref[:, :KEEP_MAX] == token_at) & (row_at < live)
    return jnp.where(hit, 1.0, 0.0).astype(BF)


def dot(a, b, contract):
    return lax.dot_general(a, b, (((contract[0],), (contract[1],)), ((), ())), preferred_element_type=F32)


def attend_kernel(info, counts, order, query, key, value, mixed, query_c, key_c, value_c, weight, pick):
    live = counts[info[0]]

    @pl.when(pl.program_id(0) == 0)
    def _():
        pick[...] = rows_by_token(order, live)

    tokens = jnp.concatenate([query[0], key[0], value[0]], axis=1)
    rows = dot(pick[...], tokens, (1, 0)).astype(BF)
    q, k, v = rows[:, :128], rows[:, 128:256], rows[:, 256:]
    query_c[...], key_c[...], value_c[...] = q, k, v
    scores = dot(q, k, (1, 1)) * HEAD_DIM ** (-0.5)
    column = lax.broadcasted_iota(jnp.int32, (KEEP_MAX, KEEP_MAX), 1)
    scores = jnp.where(column < live, scores, -1000000000.0)
    exponent = jnp.exp(scores - jnp.max(scores, axis=-1, keepdims=True))
    w = exponent / jnp.sum(exponent, axis=-1, keepdims=True)
    weight[0] = w
    mixed[...] = dot(w.astype(BF), v, (1, 0)).astype(BF)


def attend(info, counts, order, query, key, value):
    heads = query.shape[2] // HEAD_DIM
    token_spec = pl.BlockSpec((1, P_SIZE, HEAD_DIM), lambda h, *_: (0, 0, h))
    row_spec = pl.BlockSpec((KEEP_MAX, HEAD_DIM), lambda h, *_: (0, h))
    row_shape = pltpu.HBM((KEEP_MAX, heads * HEAD_DIM), BF)
    return call(
        attend_kernel, (heads,), (info, counts),
        [pl.BlockSpec((1, P_SIZE), lambda h, *_: (0, 0)), token_spec, token_spec, token_spec],
        [row_spec] * 4 + [pl.BlockSpec((1, KEEP_MAX, KEEP_MAX), lambda h, *_: (h, 0, 0))],
        [row_shape] * 4 + [pltpu.HBM((heads, KEEP_MAX, KEEP_MAX), F32)],
        [pltpu.VMEM((KEEP_MAX, P_SIZE), BF)],
        in_hbm(order), in_hbm(query), in_hbm(key), in_hbm(value), vmem=20,
    )


def attend_back_kernel(
    info, counts, order, grad, query, key, value, weight, normed, grad_q, grad_k, grad_v, normed_out, place
):
    live = counts[info[0]]

    @pl.when(pl.program_id(0) == 0)
    def _():
        place[...] = tokens_by_row(order, live)

    g, q, k, v = grad[...], query[...], key[...], value[...]
    w = weight[0]
    d_weight = dot(g, v, (1, 1)).astype(BF).astype(F32)
    inner = jnp.sum(d_weight * w, axis=-1, keepdims=True)
    d_scores = (w * (d_weight - inner) * HEAD_DIM ** (-0.5)).astype(BF)
    dq = dot(d_scores, k, (1, 0)).astype(BF)
    dk = dot(d_scores, q, (0, 0)).astype(BF)
    dv = dot(w.astype(BF), g, (0, 0)).astype(BF)
    rows = jnp.concatenate([dq, dk, dv, normed[...]], axis=1)
    out = dot(place[...], rows, (1, 0)).astype(BF)
    grad_q[0], grad_k[0], grad_v[0] = out[:, :128], out[:, 128:256], out[:, 256:384]
    normed_out[0] = out[:, 384:]


def attend_back(info, counts, order, grad, query, key, value, weight, normed):
    heads = query.shape[1] // HEAD_DIM
    width = normed.shape[1]
    token_spec = pl.BlockSpec((1, P_SIZE, HEAD_DIM), lambda h, *_: (0, 0, h))
    row_spec = pl.BlockSpec((KEEP_MAX, HEAD_DIM), lambda h, *_: (0, h))
    token_shape = jax.ShapeDtypeStruct((1, P_SIZE, heads * HEAD_DIM), BF)
    return call(
        attend_back_kernel, (heads,), (info, counts),
        [pl.BlockSpec((1, P_SIZE), lambda h, *_: (0, 0))] + [row_spec] * 4
        + [pl.BlockSpec((1, KEEP_MAX, KEEP_MAX), lambda h, *_: (h, 0, 0)),
           pl.BlockSpec((KEEP_MAX, width // heads), lambda h, *_: (0, h))],
        [token_spec] * 3 + [pl.BlockSpec((1, P_SIZE, width // heads), lambda h, *_: (0, 0, h))],
        [token_shape] * 3 + [jax.ShapeDtypeStruct((1, P_SIZE, width), BF)],
        [pltpu.VMEM((P_SIZE, KEEP_MAX), BF)],
        in_hbm(order), in_hbm(grad), in_hbm(query), in_hbm(key), in_hbm(value), in_hbm(weight), in_hbm(normed), vmem=24,
    )


def pick_kernel(info, counts, order, tokens, rows, pick):
    @pl.when(pl.program_id(0) == 0)
    def _():
        pick[...] = rows_by_token(order, counts[info[0]])

    rows[...] = dot(pick[...], tokens[0], (1, 0)).astype(BF)


def pick_rows(info, counts, order, tokens):
    width = tokens.shape[2]
    return call(
        pick_kernel, (width // 256,), (info, counts),
        [pl.BlockSpec((1, P_SIZE), lambda j, *_: (0, 0)), pl.BlockSpec((1, P_SIZE, 256), lambda j, *_: (0, 0, j))],
        pl.BlockSpec((KEEP_MAX, 256), lambda j, *_: (0, j)),
        jax.ShapeDtypeStruct((KEEP_MAX, width), BF),
        [pltpu.VMEM((KEEP_MAX, P_SIZE), BF)],
        order, tokens, vmem=12,
    )


def shift_of(y, core):
    return y if core == 0 else (8 - y if y else 4)


def cut_kernel(info, block, out):
    half = out.shape[2]
    out[0] = block[:, :half]
    out[1] = block[:, half:]


def fetch_columns(info, out_proj, chips):
    rows, full = out_proj.shape
    ranks = lax.axis_size("mp")
    width, part = full // ranks, rows // 4
    half = width // 2
    parts = call(
        cut_kernel, (1,), (info,),
        [pl.BlockSpec((part, width), lambda _, i: (i[3], lax.rem(i[1] + ranks - i[5], ranks)))],
        pl.BlockSpec((2, part, half), lambda _, i: (0, 0, 0)),
        jax.ShapeDtypeStruct((2, part, half), BF), [],
        in_hbm(out_proj), vmem=4,
    )
    table = [
        (dp_index(y, x, c) * ranks + m, dp_index(y, x, c) * ranks + (m - shift_of(y, c)) % ranks)
        for y, x, c in chips for m in range(ranks)
    ]
    got = lax.ppermute(parts, ("dp", "mp"), table)
    return got[0], got[1]


def spread_columns(parts, chips, after, beside):
    swap = [(dp_index(y, x, c), dp_index(y, x, 1 - c)) for y, x, c in chips]
    along = {
        "y": {s: [(dp_index(y, x, c), dp_index(y - s, x, c)) for y, x, c in chips] for s in STEPS[1:]},
        "x": {s: [(dp_index(y, x, c), dp_index(y, x - s, c)) for y, x, c in chips] for s in STEPS[1:]},
    }
    ways = (("y", "x"), ("x", "y"))
    first = [
        [part] + [lax.ppermute(part, "dp", along[way][s]) for s in STEPS[1:]]
        for part, (way, _) in zip(parts, ways)
    ]
    fours = [jnp.stack(pieces) for pieces in first]
    after, fours = lax.optimization_barrier((after, fours))
    done = beside(after)
    pieces = []
    for four, (_, way) in zip(fours, ways):
        for s in STEPS:
            piece = four if s == 0 else lax.ppermute(four, "dp", along[way][s])
            if way == "y" and s == STEPS[-1]:
                piece, *done = lax.optimization_barrier((piece, *done))
            pieces += [piece, lax.ppermute(piece, "dp", swap)]
    return pieces, done


def assemble_kernel(info, *refs):
    *pieces, out = refs
    ranks, rows, width = out.shape
    half, part = width // 2, rows // 4
    for stream in range(2):
        for at, second in enumerate(STEPS):
            for core in range(2):
                piece = pieces[(stream * 4 + at) * 2 + core]
                side = info[4] if core == 0 else 1 - info[4]
                for j, first in enumerate(STEPS):
                    dy, dx = (first, second) if stream == 0 else (second, first)
                    y, x = lax.rem(info[2] + 4 + dy, 4), lax.rem(info[3] + 4 + dx, 4)
                    shift = jnp.where(side == 0, y, jnp.where(y == 0, 4, 8 - y))
                    start = pl.multiple_of(x * part, 16)
                    out[lax.rem(info[1] + shift, ranks), pl.ds(start, part), stream * half:(stream + 1) * half] = piece[j]


def assemble(info, pieces, ranks):
    four, part, half = pieces[0].shape
    rows, width = four * part, 2 * half
    whole = call(
        assemble_kernel, (1,), (info,),
        [pl.BlockSpec((four, part, half), lambda _, i: (0, 0, 0))] * 16,
        pl.BlockSpec((ranks, rows, width), lambda _, i: (0, 0, 0)),
        pltpu.HBM((ranks, rows, width), BF), [],
        *pieces, vmem=24,
    )
    return whole.reshape(ranks * rows, width)


def project_kernel(info, mixed, weight, grad, gain, projected, sums):
    step = pl.program_id(0)
    part = dot(mixed[...], weight[...], (1, 0))

    @pl.when(step == 0)
    def _():
        projected[...] = part

    @pl.when(step > 0)
    def _():
        projected[...] += part

    @pl.when(step == pl.num_programs(0) - 1)
    def _():
        values = projected[...]
        scaled = grad[...].astype(F32) * gain[...].astype(F32)
        lane = lax.broadcasted_iota(jnp.int32, (KEEP_MAX, 128), 1)
        table = jnp.zeros((KEEP_MAX, 128), F32)
        for at, term in enumerate((values, values * values, scaled, scaled * values)):
            table = jnp.where(lane == at, jnp.sum(term, axis=-1, keepdims=True), table)
        sums[...] = jnp.transpose(table)[:8]


def project(info, mixed, weight, grad, gain):
    depth, width = weight.shape
    block = 1536
    return call(
        project_kernel, (depth // block,), (info,),
        [
            pl.BlockSpec((KEEP_MAX, block), lambda k, i: (0, k)),
            pl.BlockSpec((block, width), lambda k, i: (k, 0)),
            pl.BlockSpec((KEEP_MAX, width), lambda k, i: (0, 0)),
            pl.BlockSpec((1, width), lambda k, i: (0, i[1])),
        ],
        [pl.BlockSpec((KEEP_MAX, width), lambda k, i: (0, 0)), pl.BlockSpec((8, KEEP_MAX), lambda k, i: (0, 0))],
        [jax.ShapeDtypeStruct((KEEP_MAX, width), F32), jax.ShapeDtypeStruct((8, KEEP_MAX), F32)],
        [], in_hbm(mixed), in_hbm(weight), grad, gain, vmem=26,
    )


def grad_kernel(full_width, info, counts, projected, grad, gain, *refs):
    *sums, grad_proj, normed = refs
    total = sums[0][...]
    for other in sums[1:]:
        total = total + other[...]
    total = jnp.concatenate([total, jnp.zeros((120, KEEP_MAX), F32)], axis=0)
    table = jnp.transpose(total) / full_width
    row_mean, row_square, first, cross = (table[:, at:at + 1] for at in range(4))
    inv_std = lax.rsqrt(row_square - row_mean * row_mean + 1e-06)
    second = (cross - row_mean * first) * inv_std
    live = lax.broadcasted_iota(jnp.int32, (KEEP_MAX, 1), 0) < counts[info[0]]
    gain_wide = gain[...].astype(F32)
    centred = (projected[...] - row_mean) * inv_std
    scaled = grad[...].astype(F32) * gain_wide
    normed[...] = jnp.where(live, centred * gain_wide, 0.0).astype(BF)
    grad_proj[...] = jnp.where(live, inv_std * (scaled - first - centred * second), 0.0).astype(BF)


def grad_rows(info, counts, projected, grad, gain, sums, full_width):
    width = projected.shape[1]
    whole = pl.BlockSpec((KEEP_MAX, width), lambda k, *i: (0, 0))
    shape = (KEEP_MAX, width)
    return call(
        functools.partial(grad_kernel, full_width), (1,), (info, counts),
        [whole, whole, pl.BlockSpec((1, width), lambda k, i, c: (0, i[1]))]
        + [pl.BlockSpec((8, KEEP_MAX), lambda k, *i: (0, 0))] * len(sums),
        [whole, whole], [pltpu.VMEM(shape, BF), pltpu.HBM(shape, BF)],
        [], projected, grad, gain, *sums, vmem=20,
    )


def back_kernel(grad_proj, weight, out):
    product = dot(grad_proj[...], weight[...], (1, 1)).astype(BF)
    half = out.shape[2]
    out[0] = product[:, :half]
    out[1] = product[:, half:]


def project_back(grad_proj, weight):
    depth, width = weight.shape
    block = 768
    return call(
        back_kernel, (depth // block,), (),
        [pl.BlockSpec((KEEP_MAX, width), lambda k: (0, 0)), pl.BlockSpec((block, width), lambda k: (k, 0))],
        pl.BlockSpec((2, KEEP_MAX, block // 2), lambda k: (k, 0, 0)),
        pltpu.HBM((depth * 2 // block, KEEP_MAX, block // 2), BF),
        [], grad_proj, in_hbm(weight), vmem=12,
    )


def outer_kernel(info, own_grad, other_grad, own_mixed, other_mixed, out, turned):
    @pl.when(pl.program_id(0) == 0)
    def _():
        turned[:, :KEEP_MAX] = jnp.transpose(own_grad[...])
        turned[:, KEEP_MAX:] = jnp.transpose(other_grad[...])

    product = dot(turned[:, :KEEP_MAX], own_mixed[...], (1, 0))
    product = product + dot(turned[:, KEEP_MAX:], other_mixed[...], (1, 0))
    width = out.shape[2]
    for j in range(out.shape[0]):
        out[j] = product[:, j * width:(j + 1) * width].astype(BF)


def outer(info, own_grad, other_grad, mixed, other_mixed):
    width = own_grad.shape[1]
    block = mixed.shape[1] // 8
    grad_spec = pl.BlockSpec((KEEP_MAX, width), lambda j, i: (0, 0))
    mixed_spec = pl.BlockSpec((KEEP_MAX, 2 * block), lambda j, i: (0, i[4] * 2 + j))
    return call(
        outer_kernel, (2,), (info,),
        [grad_spec, grad_spec, mixed_spec, mixed_spec],
        pl.BlockSpec((2, width, block), lambda j, i: (j, 0, 0)),
        jax.ShapeDtypeStruct((4, width, block), BF),
        [pltpu.VMEM((width, 2 * KEEP_MAX), BF)],
        own_grad, other_grad, in_hbm(mixed), in_hbm(other_mixed), vmem=22,
    )


def dp_index(y, x, core):
    return (y % 4) * 8 + (x % 4) * 2 + core


def on_device(
    query_heads, key_heads, value_heads, out_proj, norm_gain, keep_order, keep_count, cotangent
):
    ranks = lax.axis_size("mp")
    image = lax.axis_index("dp")
    rank = lax.axis_index("mp")
    y_at, core = image // 8, image % 2
    shift = jnp.where(core == 0, y_at, jnp.where(y_at == 0, 4, 8 - y_at))
    info = jnp.stack([image, rank, y_at, (image // 2) % 4, core, shift]).astype(jnp.int32)
    chips = [(y, x, core) for y in range(4) for x in range(4) for core in range(2)]
    swap = [(dp_index(y, x, c), dp_index(y, x, 1 - c)) for y, x, c in chips]

    parts = fetch_columns(info, out_proj, chips)
    mixed, query_c, key_c, value_c, weights = attend(
        info, keep_count, keep_order, query_heads, key_heads, value_heads
    )
    mixed, parts = lax.optimization_barrier((mixed, parts))
    mixed_all = lax.all_gather(mixed, "mp", axis=1, tiled=True)
    pieces, (grad_c, gain) = spread_columns(
        parts, chips, info,
        lambda after: (pick_rows(after, keep_count, keep_order, cotangent), norm_gain.reshape(1, -1)),
    )
    columns = assemble(info, pieces, ranks)
    mixed_all, grad_c, columns = lax.optimization_barrier((mixed_all, grad_c, columns))
    projected, sums = project(info, mixed_all, columns, grad_c, gain)
    def swapped(values, bits):
        return lax.ppermute(values, "mp", [(m, m ^ bits) for m in range(ranks)])

    four_sums = sums + swapped(sums, 1) + swapped(sums, 3) + swapped(sums, 2)
    all_sums = [four_sums, swapped(four_sums, 7)]
    other_mixed = lax.ppermute(mixed_all, "dp", swap)
    all_sums, other_mixed = lax.optimization_barrier((all_sums, other_mixed))
    grad_proj, normed_c = grad_rows(
        info, keep_count, projected, grad_c, gain, all_sums, norm_gain.shape[0]
    )
    mixed_grad = project_back(grad_proj, columns)
    other_grad = lax.ppermute(grad_proj, "dp", swap)
    mixed_grad, other_grad = lax.optimization_barrier((mixed_grad, other_grad))
    grad_mixed = lax.psum_scatter(mixed_grad, "mp", scatter_dimension=0, tiled=True)[0]

    pair = outer(info, grad_proj, other_grad, mixed_all, other_mixed)
    width, depth = pair.shape[1], pair.shape[2]
    pair = pair.reshape(16, width // 4, depth)
    groups = [[2 * j + c for j in range(16)] for c in range(2)]
    spread = lax.all_to_all(
        pair, "dp", split_axis=0, concat_axis=0, tiled=True, axis_index_groups=groups
    )
    total = jnp.sum(spread.astype(F32), axis=0).astype(BF)
    home = [
        (dp_index(y, x, c) * ranks + m, (4 * m + x) * ranks + 4 * c + y)
        for y, x, c in chips for m in range(ranks)
    ]
    total = lax.ppermute(total, ("dp", "mp"), home)

    *grads, normed = attend_back(
        info, keep_count, keep_order, grad_mixed, query_c, key_c, value_c, weights, normed_c
    )
    total, grads = lax.optimization_barrier((total, grads))
    return (normed, *grads, total.astype(F32).T)


def solution(mesh):
    in_specs = (
        P("dp", None, "mp"),
        P("dp", None, "mp"),
        P("dp", None, "mp"),
        P("mp", None),
        P(),
        P("dp", None),
        P(),
        P("dp", None, "mp"),
    )
    out_specs = (
        P("dp", None, "mp"),
        P("dp", None, "mp"),
        P("dp", None, "mp"),
        P("dp", None, "mp"),
        P("mp", "dp"),
    )
    return jax.shard_map(
        on_device, mesh=mesh, in_specs=in_specs, out_specs=out_specs, check_vma=False
    )
```
